32 devices in a mesh: dp: 4 (over y, x), ctx: 8 (over z, core).
Axes of the slice: x: 2, y: 2, z: 4, core: 2. Of those that a mesh axis runs over, the one named last changes fastest.
Arguments:
- tokens: bfloat16 [4, 4096, 960], P('dp', 'ctx'), may hold values from -6 to 6
- positions: int32 [4, 4096], P('dp', 'ctx'), may hold values from 0 to 4095, as said below
- w_qkv: bfloat16 [960, 1600], P('dp'), may hold values from -0.12909944 to 0.12909944
- w_out: bfloat16 [960, 960], P('dp'), may hold values from -3 to 3
- w_gate: bfloat16 [960, 2560], P('dp'), may hold values from -0.1875 to 0.1875
- w_up: bfloat16 [960, 2560], P('dp'), may hold values from -0.1875 to 0.1875
- w_down: bfloat16 [2560, 960], P('dp'), may hold values from -0.125 to 0.125
- g_attn: bfloat16 [960], P('dp'), may hold values from 0.5 to 1.5
- g_mlp: bfloat16 [960], P('dp'), may hold values from 0.5 to 1.5
- grad_out: bfloat16 [4, 4096, 960], P('dp', 'ctx'), may hold values from -6 to 6
Outputs:
- output: bfloat16 [4, 4096, 960], P('dp', 'ctx')
- grad_tokens: bfloat16 [4, 4096, 960], P('dp', 'ctx')
- grad_qkv: float32 [960, 1600], P('dp')
- grad_wo: float32 [960, 960], P('dp')
- grad_gate: float32 [960, 2560], P('dp')
- grad_up: float32 [960, 2560], P('dp')
- grad_down: float32 [2560, 960], P('dp')
- grad_g_attn: float32 [960], P('dp')
- grad_g_mlp: float32 [960], P('dp')
The draws below stay inside these ranges and needn't reach their ends.
Inputs may be any that keep to these rules, and one draw needn't show every extreme that they name: In each sequence positions are a permutation of 0 to 4095: stored tokens in rows r * 512 to (r + 1) * 512 - 1 hold two runs of 256 consecutive positions in rising order, position blocks b and 15 - b of 256 positions each, with b differing from r to r.
All inputs are finite; a program needn't handle non-finite values.
Results may differ from the reference program's by a relative error of at most 0.023.
Values may be sent and summed in bfloat16 or wider, within the bound.
No kernel may reach another device: no remote copies, remote signals or barrier semaphores. Data moves between devices by JAX's collectives and lax.ppermute only.
A program may use at most 256 MiB of HBM per device.

```python
import jax
import jax.numpy as jnp
from jax import lax

D = 960
QUERY_HEADS = 15
KEY_VALUE_HEADS = 5
HEAD_SIZE = 64
FF = 2560
TOKENS_PER_SHARD = 512
SEQUENCE_LENGTH = 4096
SEQS = 4


def draw_positions(key, part):
    ranks = SEQUENCE_LENGTH // TOKENS_PER_SHARD
    half_rows = TOKENS_PER_SHARD // 2
    keys_list = jax.random.split(key, SEQS)

    def one_sequence(seq_key):
        block_order = jax.random.permutation(seq_key, ranks)
        slot_index = jnp.arange(SEQUENCE_LENGTH)
        owner_rank = slot_index // TOKENS_PER_SHARD
        within = slot_index % TOKENS_PER_SHARD
        first_half = within < half_rows
        chosen = block_order[owner_rank]
        block_of = jnp.where(first_half, chosen, 2 * ranks - 1 - chosen)
        return (block_of * half_rows + within % half_rows).astype(jnp.int32)
    return jax.vmap(one_sequence)(keys_list)


def draw_tokens(key, part):
    noise_key = jax.random.fold_in(key, 11)
    values = jnp.clip(jax.random.normal(noise_key, (SEQS, SEQUENCE_LENGTH, D), jnp.float32), -6.0, 6.0)
    return values.astype(jnp.bfloat16)


def draw_w_qkv(key, part):
    total_column_count = (QUERY_HEADS + 2 * KEY_VALUE_HEADS) * HEAD_SIZE
    base_key = jax.random.fold_in(key, 21)
    values = jnp.clip(jax.random.normal(base_key, (D, total_column_count), jnp.float32), -4.0, 4.0)
    return (values * D ** (-0.5)).astype(jnp.bfloat16)


def levels(rng, dims, cuts, least, high):
    level = 1.0
    for position, blocks in cuts:
        heights = jax.random.uniform(jax.random.fold_in(jax.random.fold_in(rng, 6), position), (blocks,), jnp.float32, least / len(cuts), high / len(cuts))
        level = level * jnp.repeat(jnp.exp(heights), dims[position] // blocks).reshape((-1,) + (1,) * (len(dims) - 1 - position))
    return level


def scatter_about(own_key, dims, deviation, bound, cuts=(), held_as=jnp.bfloat16):
    values = jax.random.normal(own_key, dims, jnp.float32) * deviation
    if len(cuts) > 0:
        values = levels(own_key, dims, cuts, -0.22, 0.18) * values
    return jnp.clip(values, min=-bound, max=bound).astype(held_as)


def setup_inputs(seed: int = 0) -> dict:
    key_list = jax.random.split(jax.random.key(seed), 11)
    tokens = draw_tokens(jax.random.fold_in(key_list[10], 71), 0)
    positions = draw_positions(jax.random.fold_in(key_list[10], 71), 0)
    w_qkv = draw_w_qkv(jax.random.fold_in(key_list[10], 71), 0)
    w_out = scatter_about(key_list[3], (QUERY_HEADS * HEAD_SIZE, D), 4 ** -0.5, 3.0, ((0, 4),))
    w_gate = scatter_about(key_list[4], (D, FF), D ** -0.5, 0.1875, ((0, 4),))
    w_up = scatter_about(key_list[5], (D, FF), D ** -0.5, 0.1875, ((0, 4),))
    w_down = scatter_about(key_list[6], (FF, D), FF ** -0.5, 0.125, ((0, 4),))
    g_attn = jnp.clip(1.0 + 0.1 * jax.random.normal(key_list[7], (D,), jnp.float32), 0.5, 1.5).astype(jnp.bfloat16)
    g_mlp = jnp.clip(1.0 + 0.1 * jax.random.normal(key_list[8], (D,), jnp.float32), 0.5, 1.5).astype(jnp.bfloat16)
    grad_out = scatter_about(key_list[9], (SEQS, SEQUENCE_LENGTH, D), 1.0, 6.0, ((0, 4), (1, 8)))
    return dict(tokens=tokens, positions=positions, w_qkv=w_qkv, w_out=w_out, w_gate=w_gate, w_up=w_up, w_down=w_down, g_attn=g_attn, g_mlp=g_mlp, grad_out=grad_out)


EPS = 1e-05
THETA = 10000.0
MASK_FILL = -1e+30

def rope_tables(seq_pos, head_dim):
    half_dim = head_dim // 2
    freqs = THETA ** (-(jnp.arange(half_dim).astype(jnp.float32) * 2.0) / head_dim)
    angles = seq_pos.astype(jnp.float32)[:, None] * freqs[None, :]
    angles = jnp.concatenate([angles, angles], axis=1)
    return (jnp.cos(angles)[:, None, :], jnp.sin(angles)[:, None, :])

def apply_rotation(values, cosine_table, sine_table):
    half_dim = values.shape[-1] // 2
    turned = jnp.concatenate([-values[..., half_dim:], values[..., :half_dim]], axis=-1)
    return values * cosine_table + turned * sine_table

def unrotate(grads, cosine_table, sine_table):
    half_dim = grads.shape[-1] // 2
    moved = grads * sine_table
    turned = jnp.concatenate([moved[..., half_dim:], -moved[..., :half_dim]], axis=-1)
    return grads * cosine_table + turned

def norm_forward(inputs, gain):
    factor = lax.rsqrt(lax.optimization_barrier(jnp.mean(inputs * inputs, axis=-1, keepdims=True)) + EPS)
    return (factor, (inputs * factor * gain.astype(jnp.float32)).astype(jnp.bfloat16))

def norm_backward(inputs, factor, gain, grad_normed):
    scaled = grad_normed * gain.astype(jnp.float32)
    grad_inputs = factor * scaled - inputs * factor ** 3 * lax.optimization_barrier(jnp.mean(scaled * inputs, axis=-1, keepdims=True))
    grad_gain = lax.optimization_barrier(jnp.sum(grad_normed * inputs * factor, axis=0))
    return (grad_inputs, grad_gain)

def scores_of(query_rows, query_pos, key_part, key_pos):
    products = jnp.einsum('bkgh,nkh->kgbn', query_rows.astype(jnp.float32), key_part.astype(jnp.float32)) * HEAD_SIZE ** (-0.5)
    allowed = key_pos[None, :] <= query_pos[:, None]
    return jnp.where(allowed[None, None], products, MASK_FILL)

def sequence_pass(inputs, seq_pos, seq_grad, weights):
    w_qkv, w_out, w_gate, w_up, w_down, g_attn, g_mlp = weights
    query_groups = QUERY_HEADS // KEY_VALUE_HEADS
    query_width = QUERY_HEADS * HEAD_SIZE
    key_value_width = KEY_VALUE_HEADS * HEAD_SIZE
    block_count = SEQUENCE_LENGTH // TOKENS_PER_SHARD
    scaling = HEAD_SIZE ** (-0.5)
    resid_in = inputs.astype(jnp.float32)
    factor_one, normed_one = norm_forward(resid_in, g_attn)
    projection_result = jnp.dot(normed_one, w_qkv, preferred_element_type=jnp.float32)
    cosine_table, sine_table = rope_tables(seq_pos, HEAD_SIZE)
    query_rows = apply_rotation(projection_result[:, :query_width].reshape(SEQUENCE_LENGTH, QUERY_HEADS, HEAD_SIZE), cosine_table, sine_table).astype(jnp.bfloat16)
    every_key = apply_rotation(projection_result[:, query_width:query_width + key_value_width].reshape(SEQUENCE_LENGTH, KEY_VALUE_HEADS, HEAD_SIZE), cosine_table, sine_table).astype(jnp.bfloat16)
    every_value = projection_result[:, query_width + key_value_width:].reshape(SEQUENCE_LENGTH, KEY_VALUE_HEADS, HEAD_SIZE).astype(jnp.bfloat16)
    blocked_queries = query_rows.reshape(block_count, TOKENS_PER_SHARD, KEY_VALUE_HEADS, query_groups, HEAD_SIZE)
    pos_blocks = seq_pos.reshape(block_count, TOKENS_PER_SHARD)

    def attend(packed):
        query_blk, query_pos = packed
        scores = scores_of(query_blk, query_pos, every_key, seq_pos)
        row_max = lax.optimization_barrier(jnp.max(scores, axis=-1, keepdims=True))
        log_sum = row_max + jnp.log(lax.optimization_barrier(jnp.sum(jnp.exp(scores - row_max), axis=-1, keepdims=True)))
        probs = jnp.exp(scores - log_sum)
        mixed = jnp.einsum('kgbn,nkh->bkgh', probs, every_value.astype(jnp.float32))
        return (mixed.astype(jnp.bfloat16), log_sum[..., 0])
    attn_blocks, lse_blocks = lax.map(attend, (blocked_queries, pos_blocks))
    attention_result = attn_blocks.reshape(SEQUENCE_LENGTH, query_width)
    resid_mid = resid_in + jnp.dot(attention_result, w_out, preferred_element_type=jnp.float32)
    factor_two, normed_two = norm_forward(resid_mid, g_mlp)
    gate_pre = jnp.dot(normed_two, w_gate, preferred_element_type=jnp.float32)
    upward = jnp.dot(normed_two, w_up, preferred_element_type=jnp.float32)
    sigmoid_gate = jax.nn.sigmoid(gate_pre)
    activated = (gate_pre * sigmoid_gate * upward).astype(jnp.bfloat16)
    output = (resid_mid + jnp.dot(activated, w_down, preferred_element_type=jnp.float32)).astype(jnp.bfloat16)
    grad_top = seq_grad.astype(jnp.float32)
    grad_down_w = jnp.dot(activated.T, seq_grad, preferred_element_type=jnp.float32)
    grad_act = jnp.dot(seq_grad, w_down.T, preferred_element_type=jnp.float32)
    grad_gate_rows = (grad_act * upward * sigmoid_gate * (1.0 + gate_pre * (1.0 - sigmoid_gate))).astype(jnp.bfloat16)
    grad_up_rows = (grad_act * gate_pre * sigmoid_gate).astype(jnp.bfloat16)
    grad_gate_w = jnp.dot(normed_two.T, grad_gate_rows, preferred_element_type=jnp.float32)
    grad_up_w = jnp.dot(normed_two.T, grad_up_rows, preferred_element_type=jnp.float32)
    grad_normed_two = jnp.dot(grad_gate_rows, w_gate.T, preferred_element_type=jnp.float32) + jnp.dot(grad_up_rows, w_up.T, preferred_element_type=jnp.float32)
    grad_mid, grad_gain_mlp = norm_backward(resid_mid, factor_two, g_mlp, grad_normed_two)
    grad_mid = grad_mid + grad_top
    grad_mid_half = grad_mid.astype(jnp.bfloat16)
    grad_out_w = jnp.dot(attention_result.T, grad_mid_half, preferred_element_type=jnp.float32)
    head_gradients = jnp.dot(grad_mid_half, w_out.T, preferred_element_type=jnp.float32).astype(jnp.bfloat16)
    block_gradients = head_gradients.reshape(block_count, TOKENS_PER_SHARD, KEY_VALUE_HEADS, query_groups, HEAD_SIZE)

    def attend_back(key_grads, packed):
        query_blk, query_pos, attn_blk, grad_blk, log_sum = packed
        grad_key_acc, grad_value_acc = key_grads
        scores = scores_of(query_blk, query_pos, every_key, seq_pos)
        probs = jnp.exp(scores - log_sum[..., None])
        grad_float = grad_blk.astype(jnp.float32)
        delta = jnp.einsum('bkgh,bkgh->kgb', grad_float, attn_blk.astype(jnp.float32))
        grad_probs = jnp.einsum('bkgh,nkh->kgbn', grad_float, every_value.astype(jnp.float32))
        grad_scores = (probs * (grad_probs - delta[..., None])).astype(jnp.bfloat16).astype(jnp.float32)
        grad_query = jnp.einsum('kgbn,nkh->bkgh', grad_scores, every_key.astype(jnp.float32)) * scaling
        grad_key = jnp.einsum('kgbn,bkgh->nkh', grad_scores, query_blk.astype(jnp.float32)) * scaling
        probs_half = lax.optimization_barrier(probs.astype(jnp.bfloat16)).astype(jnp.float32)
        grad_value = jnp.einsum('kgbn,bkgh->nkh', probs_half, grad_float)
        return ((grad_key_acc + grad_key, grad_value_acc + grad_value), grad_query)
    empty_key_rows = jnp.zeros((SEQUENCE_LENGTH, KEY_VALUE_HEADS, HEAD_SIZE), jnp.float32)
    (grad_keys, grad_values), grad_queries = lax.scan(attend_back, (empty_key_rows, empty_key_rows), (blocked_queries, pos_blocks, attn_blocks, block_gradients, lse_blocks))
    grad_q_rows = unrotate(grad_queries.reshape(SEQUENCE_LENGTH, QUERY_HEADS, HEAD_SIZE), cosine_table, sine_table).reshape(SEQUENCE_LENGTH, query_width)
    grad_k_rows = unrotate(grad_keys, cosine_table, sine_table).reshape(SEQUENCE_LENGTH, key_value_width)
    grad_proj = jnp.concatenate([grad_q_rows, grad_k_rows, grad_values.reshape(SEQUENCE_LENGTH, key_value_width)], axis=1).astype(jnp.bfloat16)
    grad_qkv_w = jnp.dot(normed_one.T, grad_proj, preferred_element_type=jnp.float32)
    grad_normed_one = jnp.dot(grad_proj, w_qkv.T, preferred_element_type=jnp.float32)
    grad_in, grad_gain_attn = norm_backward(resid_in, factor_one, g_attn, grad_normed_one)
    grad_in = (grad_in + grad_mid).astype(jnp.bfloat16)
    return (output, grad_in, (grad_qkv_w, grad_out_w, grad_gate_w, grad_up_w, grad_down_w, grad_gain_attn, grad_gain_mlp))

def reference(tokens, positions, w_qkv, w_out, w_gate, w_up, w_down, g_attn, g_mlp, grad_out):
    weights = (w_qkv, w_out, w_gate, w_up, w_down, g_attn, g_mlp)
    zero_filled = jax.tree.map(lambda weight_leaf: jnp.zeros(weight_leaf.shape, jnp.float32), weights)

    def one_sequence(totals, packed):
        inputs, seq_pos, seq_grad = packed
        output, grad_in, grads = sequence_pass(inputs, seq_pos, seq_grad, weights)
        return (jax.tree.map(jnp.add, totals, grads), (output, grad_in))
    totals, (outputs, grads_in) = lax.scan(one_sequence, zero_filled, (tokens, positions, grad_out))
    return (outputs, grads_in, totals[0], totals[1], totals[2], totals[3], totals[4], totals[5], totals[6])
```

```python
import functools

import jax
import jax.numpy as jnp
from jax import lax
from jax.experimental import pallas as pl
from jax.experimental.pallas import tpu as pltpu
from jax.sharding import PartitionSpec as P

QUERY_HEADS = 15
KEY_VALUE_HEADS = 5
HEAD_SIZE = 64
GROUPS = QUERY_HEADS // KEY_VALUE_HEADS


EPS = 1e-05
THETA = 10000.0
MASK_FILL = -1e30


def rope_tables(seq_pos, head_dim):
    half_dim = head_dim // 2
    freqs = THETA ** (-(jnp.arange(half_dim).astype(jnp.float32) * 2.0) / head_dim)
    angles = seq_pos.astype(jnp.float32)[:, None] * freqs[None, :]
    angles = jnp.concatenate([angles, angles], axis=1)
    return (jnp.cos(angles)[:, None, :], jnp.sin(angles)[:, None, :])


def apply_rotation(values, cosine_table, sine_table):
    half_dim = values.shape[-1] // 2
    turned = jnp.concatenate([-values[..., half_dim:], values[..., :half_dim]], axis=-1)
    return values * cosine_table + turned * sine_table


def unrotate(grads, cosine_table, sine_table):
    half_dim = grads.shape[-1] // 2
    moved = grads * sine_table
    turned = jnp.concatenate([moved[..., half_dim:], -moved[..., :half_dim]], axis=-1)
    return grads * cosine_table + turned


def norm_forward(inputs, gain):
    factor = lax.rsqrt(jnp.mean(inputs * inputs, axis=-1, keepdims=True) + EPS)
    return (factor, (inputs * factor * gain.astype(jnp.float32)).astype(jnp.bfloat16))


def norm_backward(inputs, factor, gain, grad_normed):
    scaled = grad_normed * gain.astype(jnp.float32)
    grad_inputs = factor * scaled - inputs * factor**3 * jnp.mean(
        scaled * inputs, axis=-1, keepdims=True
    )
    grad_gain = jnp.sum(grad_normed * inputs * factor, axis=0)
    return (grad_inputs, grad_gain)


def list_pairs(qblk, kblk, lst, nblk):
    cnt=jnp.int32(0)
    for r in range(2):
        def body(j,c,r=r):
            act=kblk[j]<qblk[r]
            @pl.when(act)
            def _():
                lst[c]=r*256+j
            return c+act.astype(jnp.int32)
        cnt=lax.fori_loop(0,nblk,body,cnt)
    return cnt

def forward_kernel(nblk, run, qblk, kblk, own, qT, kv, oT, lse, m_s, l_s, acc_s, lst):
    list_pairs(qblk,kblk,lst,nblk)
    tri=lax.broadcasted_iota(jnp.int32,(run,run),0)<=lax.broadcasted_iota(jnp.int32,(run,run),1)
    def pair(rank,ko,qo,diag):
        def sdot(hd):
            h=hd//GROUPS
            k=kv[rank,h*HEAD_SIZE:(h+1)*HEAD_SIZE,pl.ds(ko,run)].T
            q=qT[hd*HEAD_SIZE:(hd+1)*HEAD_SIZE,pl.ds(qo,run)]
            return jnp.dot(k,q,preferred_element_type=jnp.float32)
        if not diag:
            mo_all=m_s[:,pl.ds(qo,run)]
            lo_all=l_s[:,pl.ds(qo,run)]
        ms=[];ls=[]
        nxt=sdot(0)
        pend=None
        def flush(pend):
            hd,p,al=pend
            h=hd//GROUPS
            vT=kv[rank,(KEY_VALUE_HEADS+h)*HEAD_SIZE:(KEY_VALUE_HEADS+h+1)*HEAD_SIZE,pl.ds(ko,run)]
            o=jnp.dot(vT,p,preferred_element_type=jnp.float32)
            if al is None: acc_s[hd*HEAD_SIZE:(hd+1)*HEAD_SIZE,pl.ds(qo,run)]=o
            else: acc_s[hd*HEAD_SIZE:(hd+1)*HEAD_SIZE,pl.ds(qo,run)]=acc_s[hd*HEAD_SIZE:(hd+1)*HEAD_SIZE,pl.ds(qo,run)]*al+o
        def mx(hd,s):
            if diag: s=jnp.where(tri,s,MASK_FILL)
            mn=jnp.max(s,axis=0,keepdims=True)
            if not diag: mn=jnp.maximum(mo_all[hd:hd+1],mn)
            return s,mn
        s1=sdot(1)
        cur=mx(0,nxt)
        for hd in range(QUERY_HEADS):
            s,mn=cur
            if hd+1<QUERY_HEADS:
                cur=mx(hd+1,s1)
            if hd+2<QUERY_HEADS: s1=sdot(hd+2)
            if pend is not None: flush(pend)
            p=jnp.exp(s-mn)
            if diag:
                al=None; l=jnp.sum(p,axis=0,keepdims=True)
            else:
                al=jnp.exp(mo_all[hd:hd+1]-mn)
                l=lo_all[hd:hd+1]*al+jnp.sum(p,axis=0,keepdims=True)
            ms.append(mn); ls.append(l)
            pend=(hd,p.astype(jnp.bfloat16),al)
        flush(pend)
        m_s[:,pl.ds(qo,run)]=jnp.concatenate(ms+[ms[-1]],0)
        l_s[:,pl.ds(qo,run)]=jnp.concatenate(ls+[ls[-1]],0)
    for r in range(2):
        pair(own[0],r*run,r*run,True)
    def body(i,_):
        c=lst[i]
        r=c//256; j=c%256
        pair(j//2,pl.multiple_of((j%2)*run,run),pl.multiple_of(r*run,run),False)
        return 0
    lax.fori_loop(0,nblk-1,body,0)
    lse[...]=m_s[...]+jnp.log(l_s[...])
    for hd in range(QUERY_HEADS):
        oT[hd*HEAD_SIZE:(hd+1)*HEAD_SIZE,:]=(acc_s[hd*HEAD_SIZE:(hd+1)*HEAD_SIZE,:]/l_s[hd:hd+1,:]).astype(jnp.bfloat16)

def attention_forward(qblk,kblk,own,qT,kv):
    n=kv.shape[0]; T=qT.shape[1]; run=T//2
    sm=pl.BlockSpec(memory_space=pltpu.SMEM); vm=pl.BlockSpec(memory_space=pltpu.VMEM)
    return pl.pallas_call(functools.partial(forward_kernel,2*n,run),
        out_shape=(jax.ShapeDtypeStruct((QUERY_HEADS*HEAD_SIZE,T),jnp.bfloat16),jax.ShapeDtypeStruct((16,T),jnp.float32)),
        in_specs=[sm,sm,sm,vm,vm],out_specs=(vm,vm),
        scratch_shapes=[pltpu.VMEM((16,T),jnp.float32),pltpu.VMEM((16,T),jnp.float32),pltpu.VMEM((QUERY_HEADS*HEAD_SIZE,T),jnp.float32),pltpu.SMEM((4*n,),jnp.int32)],
        compiler_params=pltpu.CompilerParams(vmem_limit_bytes=60*2**20),name="attn_fwd")(qblk,kblk,own,qT,kv)

def backward_kernel(nblk, run, qblk, kblk, own, qT, kv, oT, lse, doT, dqT, dkv, dq_s, dkv_s, dl_s, lst):
    list_pairs(qblk,kblk,lst,nblk)
    tri=lax.broadcasted_iota(jnp.int32,(run,run),0)<=lax.broadcasted_iota(jnp.int32,(run,run),1)
    dkv_s[...]=jnp.zeros_like(dkv_s)
    dq_s[...]=jnp.zeros_like(dq_s)
    for hd in range(QUERY_HEADS):
        dl_s[hd:hd+1,:]=jnp.sum(oT[hd*HEAD_SIZE:(hd+1)*HEAD_SIZE,:].astype(jnp.float32)*doT[hd*HEAD_SIZE:(hd+1)*HEAD_SIZE,:].astype(jnp.float32),axis=0,keepdims=True)
    nt=(((1,),(1,)),((),()))
    def pair(rank,ko,qo,diag):
        ls_all=lse[:,pl.ds(qo,run)]
        dl_all=dl_s[:,pl.ds(qo,run)]
        def first(hd):
            h=hd//GROUPS
            k=kv[rank,h*HEAD_SIZE:(h+1)*HEAD_SIZE,pl.ds(ko,run)].T
            v=kv[rank,(KEY_VALUE_HEADS+h)*HEAD_SIZE:(KEY_VALUE_HEADS+h+1)*HEAD_SIZE,pl.ds(ko,run)].T
            q=qT[hd*HEAD_SIZE:(hd+1)*HEAD_SIZE,pl.ds(qo,run)]
            do=doT[hd*HEAD_SIZE:(hd+1)*HEAD_SIZE,pl.ds(qo,run)]
            return jnp.dot(k,q,preferred_element_type=jnp.float32),jnp.dot(v,do,preferred_element_type=jnp.float32)
        def last(hd,p,ds):
            h=hd//GROUPS
            q=qT[hd*HEAD_SIZE:(hd+1)*HEAD_SIZE,pl.ds(qo,run)]
            do=doT[hd*HEAD_SIZE:(hd+1)*HEAD_SIZE,pl.ds(qo,run)]
            kT=kv[rank,h*HEAD_SIZE:(h+1)*HEAD_SIZE,pl.ds(ko,run)]
            dkv_s[rank,(KEY_VALUE_HEADS+h)*HEAD_SIZE:(KEY_VALUE_HEADS+h+1)*HEAD_SIZE,pl.ds(ko,run)]+=lax.dot_general(do,p,nt,preferred_element_type=jnp.float32)
            dkv_s[rank,h*HEAD_SIZE:(h+1)*HEAD_SIZE,pl.ds(ko,run)]+=lax.dot_general(q,ds,nt,preferred_element_type=jnp.float32)
            dq_s[hd*HEAD_SIZE:(hd+1)*HEAD_SIZE,pl.ds(qo,run)]+=jnp.dot(kT,ds,preferred_element_type=jnp.float32)
        nxt=first(0); pend=None
        for hd in range(QUERY_HEADS):
            s,dp=nxt
            if hd+1<QUERY_HEADS: nxt=first(hd+1)
            if pend is not None: last(*pend)
            p=jnp.exp(s-ls_all[hd:hd+1])
            if diag: p=jnp.where(tri,p,0.0)
            ds=(p*(dp-dl_all[hd:hd+1])).astype(jnp.bfloat16)
            pend=(hd,p.astype(jnp.bfloat16),ds)
        last(*pend)
    for r in range(2):
        pair(own[0],r*run,r*run,True)
    def body(i,_):
        c=lst[i]
        r=c//256; j=c%256
        pair(j//2,pl.multiple_of((j%2)*run,run),pl.multiple_of(r*run,run),False)
        return 0
    lax.fori_loop(0,nblk-1,body,0)
    dqT[...]=dq_s[...]*(HEAD_SIZE**-0.5)
    dkv[...]=dkv_s[...].astype(jnp.bfloat16)

def attention_backward(qblk,kblk,own,qT,kv,oT,lse,doT):
    n=kv.shape[0]; T=qT.shape[1]; run=T//2
    sm=pl.BlockSpec(memory_space=pltpu.SMEM); vm=pl.BlockSpec(memory_space=pltpu.VMEM)
    return pl.pallas_call(functools.partial(backward_kernel,2*n,run),
        out_shape=(jax.ShapeDtypeStruct((QUERY_HEADS*HEAD_SIZE,T),jnp.float32),jax.ShapeDtypeStruct(kv.shape,jnp.bfloat16)),
        in_specs=[sm,sm,sm,vm,vm,vm,vm,vm],out_specs=(vm,vm),
        scratch_shapes=[pltpu.VMEM((QUERY_HEADS*HEAD_SIZE,T),jnp.float32),pltpu.VMEM(kv.shape,jnp.float32),pltpu.VMEM((16,T),jnp.float32),pltpu.SMEM((4*n,),jnp.int32)],
        compiler_params=pltpu.CompilerParams(vmem_limit_bytes=60*2**20),name="attn_bwd")(qblk,kblk,own,qT,kv,oT,lse,doT)
def local(tokens, positions, w_qkv, w_out, w_gate, w_up, w_down, g_attn, g_mlp, grad_out):
    full_qkv, full_out, full_gate, full_up, full_down, gain_attn, gain_mlp = (
        lax.all_gather(w_qkv, "dp", axis=0, tiled=True),
        lax.all_gather(w_out, "dp", axis=0, tiled=True),
        lax.all_gather(w_gate, "dp", axis=0, tiled=True),
        lax.all_gather(w_up, "dp", axis=0, tiled=True),
        lax.all_gather(w_down, "dp", axis=0, tiled=True),
        lax.all_gather(g_attn, "dp", axis=0, tiled=True),
        lax.all_gather(g_mlp, "dp", axis=0, tiled=True),
    )
    shard_rows = tokens.shape[1]
    query_groups = QUERY_HEADS // KEY_VALUE_HEADS
    query_width = QUERY_HEADS * HEAD_SIZE
    key_value_width = KEY_VALUE_HEADS * HEAD_SIZE
    scaling = HEAD_SIZE ** (-0.5)
    seq_pos = positions[0]
    resid_in = tokens[0].astype(jnp.float32)
    factor_one, normed_one = norm_forward(resid_in, gain_attn)
    projection_result = jnp.dot(normed_one, full_qkv, preferred_element_type=jnp.float32)
    cosine_table, sine_table = rope_tables(seq_pos, HEAD_SIZE)
    query_rows = apply_rotation(
        projection_result[:, :query_width].reshape(shard_rows, QUERY_HEADS, HEAD_SIZE),
        cosine_table,
        sine_table,
    ).astype(jnp.bfloat16)
    query_t = (query_rows.reshape(shard_rows, query_width) * jnp.bfloat16(scaling)).T
    key_part = apply_rotation(
        projection_result[:, query_width : query_width + key_value_width].reshape(
            shard_rows, KEY_VALUE_HEADS, HEAD_SIZE
        ),
        cosine_table,
        sine_table,
    ).astype(jnp.bfloat16)
    value_part = projection_result[:, query_width + key_value_width :].astype(jnp.bfloat16)
    key_vals = jnp.concatenate([key_part.reshape(shard_rows, key_value_width), value_part], axis=1)
    run = shard_rows // 2
    all_kv = lax.all_gather(key_vals.T, "ctx", axis=0)
    query_blocks = seq_pos[::run] // run
    key_blocks = lax.all_gather(query_blocks, "ctx", axis=0, tiled=True)
    own = lax.axis_index("ctx").astype(jnp.int32)[None]
    attention_t, log_sum = attention_forward(query_blocks, key_blocks, own, query_t, all_kv)
    attention_result = attention_t.T
    resid_mid = resid_in + jnp.dot(attention_result, full_out, preferred_element_type=jnp.float32)
    factor_two, normed_two = norm_forward(resid_mid, gain_mlp)
    gate_pre = jnp.dot(normed_two, full_gate, preferred_element_type=jnp.float32)
    upward = jnp.dot(normed_two, full_up, preferred_element_type=jnp.float32)
    sigmoid_gate = jax.nn.sigmoid(gate_pre)
    activated = (gate_pre * sigmoid_gate * upward).astype(jnp.bfloat16)
    output = (resid_mid + jnp.dot(activated, full_down, preferred_element_type=jnp.float32)).astype(
        jnp.bfloat16
    )
    back_qkv, back_out, back_gate, back_up, back_down, back_gain_attn, back_gain_mlp = (
        full_qkv,
        full_out,
        full_gate,
        full_up,
        full_down,
        gain_attn,
        gain_mlp,
    )
    grad_top = grad_out[0]
    grad_act = jnp.einsum("td,fd->tf", grad_top, back_down, preferred_element_type=jnp.float32)
    grad_gate_rows = (
        grad_act * upward * sigmoid_gate * (1.0 + gate_pre * (1.0 - sigmoid_gate))
    ).astype(jnp.bfloat16)
    grad_up_rows = (grad_act * gate_pre * sigmoid_gate).astype(jnp.bfloat16)
    grad_normed_two = jnp.einsum(
        "tf,df->td", grad_gate_rows, back_gate, preferred_element_type=jnp.float32
    ) + jnp.einsum("tf,df->td", grad_up_rows, back_up, preferred_element_type=jnp.float32)
    grad_mid, grad_gain_mlp = norm_backward(resid_mid, factor_two, back_gain_mlp, grad_normed_two)
    grad_mid = grad_mid + grad_top.astype(jnp.float32)
    grad_mid_half = grad_mid.astype(jnp.bfloat16)
    head_gradients = jnp.einsum(
        "td,cd->tc", grad_mid_half, back_out, preferred_element_type=jnp.float32
    ).astype(jnp.bfloat16)
    grad_query_t, grad_kv = attention_backward(
        query_blocks, key_blocks, own, query_t, all_kv, attention_t, log_sum, head_gradients.T
    )
    grad_query = grad_query_t.T
    local_key_value_gradient = lax.psum_scatter(
        grad_kv, "ctx", scatter_dimension=0, tiled=False
    ).astype(jnp.float32).T
    grad_q_rows = unrotate(
        grad_query.reshape(shard_rows, QUERY_HEADS, HEAD_SIZE), cosine_table, sine_table
    ).reshape(shard_rows, query_width)
    grad_k_rows = unrotate(
        local_key_value_gradient[:, :key_value_width].reshape(
            shard_rows, KEY_VALUE_HEADS, HEAD_SIZE
        ),
        cosine_table,
        sine_table,
    ).reshape(shard_rows, key_value_width)
    grad_proj = jnp.concatenate(
        [grad_q_rows, grad_k_rows, local_key_value_gradient[:, key_value_width:]], axis=1
    ).astype(jnp.bfloat16)
    grad_normed_one = jnp.einsum(
        "tc,dc->td", grad_proj, back_qkv, preferred_element_type=jnp.float32
    )
    grad_in, grad_gain_attn = norm_backward(resid_in, factor_one, back_gain_attn, grad_normed_one)
    grad_in = (grad_in + grad_mid).astype(jnp.bfloat16)
    term_qkv = jnp.einsum("td,tc->dc", normed_one, grad_proj, preferred_element_type=jnp.float32)
    term_out = jnp.einsum(
        "tc,td->cd", attention_result, grad_mid_half, preferred_element_type=jnp.float32
    )
    term_gate = jnp.einsum(
        "td,tf->df", normed_two, grad_gate_rows, preferred_element_type=jnp.float32
    )
    term_up = jnp.einsum("td,tf->df", normed_two, grad_up_rows, preferred_element_type=jnp.float32)
    term_down = jnp.einsum("tf,td->fd", activated, grad_top, preferred_element_type=jnp.float32)
    share_qkv, share_out, share_gate, share_up, share_down, share_attn, share_mlp = (
        lax.psum_scatter(
            term_qkv.astype(jnp.bfloat16), "dp", scatter_dimension=0, tiled=True
        ).astype(jnp.float32),
        lax.psum_scatter(
            term_out.astype(jnp.bfloat16), "dp", scatter_dimension=0, tiled=True
        ).astype(jnp.float32),
        lax.psum_scatter(
            term_gate.astype(jnp.bfloat16), "dp", scatter_dimension=0, tiled=True
        ).astype(jnp.float32),
        lax.psum_scatter(
            term_up.astype(jnp.bfloat16), "dp", scatter_dimension=0, tiled=True
        ).astype(jnp.float32),
        lax.psum_scatter(
            term_down.astype(jnp.bfloat16), "dp", scatter_dimension=0, tiled=True
        ).astype(jnp.float32),
        lax.psum_scatter(
            grad_gain_attn.astype(jnp.bfloat16), "dp", scatter_dimension=0, tiled=True
        ).astype(jnp.float32),
        lax.psum_scatter(
            grad_gain_mlp.astype(jnp.bfloat16), "dp", scatter_dimension=0, tiled=True
        ).astype(jnp.float32),
    )
    total_qkv, total_out, total_gate, total_up, total_down, total_attn, total_mlp = (
        lax.psum(share_qkv.astype(jnp.bfloat16), "ctx").astype(jnp.float32),
        lax.psum(share_out.astype(jnp.bfloat16), "ctx").astype(jnp.float32),
        lax.psum(share_gate.astype(jnp.bfloat16), "ctx").astype(jnp.float32),
        lax.psum(share_up.astype(jnp.bfloat16), "ctx").astype(jnp.float32),
        lax.psum(share_down.astype(jnp.bfloat16), "ctx").astype(jnp.float32),
        lax.psum(share_attn.astype(jnp.bfloat16), "ctx").astype(jnp.float32),
        lax.psum(share_mlp.astype(jnp.bfloat16), "ctx").astype(jnp.float32),
    )
    return (
        output[None],
        grad_in[None],
        total_qkv,
        total_out,
        total_gate,
        total_up,
        total_down,
        total_attn,
        total_mlp,
    )


def solution(mesh):
    placed = (
        P("dp", "ctx", None),
        P("dp", "ctx"),
        P("dp", None),
        P("dp", None),
        P("dp", None),
        P("dp", None),
        P("dp", None),
        P("dp"),
        P("dp"),
        P("dp", "ctx", None),
    )
    return jax.shard_map(
        local,
        mesh=mesh,
        in_specs=placed,
        out_specs=(
            P("dp", "ctx", None),
            P("dp", "ctx", None),
            P("dp", None),
            P("dp", None),
            P("dp", None),
            P("dp", None),
            P("dp", None),
            P("dp"),
            P("dp"),
        ),
        check_vma=False,
    )
```

```python
import functools

import jax
import jax.numpy as jnp
from jax import lax
from jax.experimental import pallas as pl
from jax.experimental.pallas import tpu as pltpu
from jax.sharding import PartitionSpec as P

QUERY_HEADS = 15
KEY_VALUE_HEADS = 5
HEAD_SIZE = 64
GROUPS = QUERY_HEADS // KEY_VALUE_HEADS
QW = QUERY_HEADS * HEAD_SIZE
KW = KEY_VALUE_HEADS * HEAD_SIZE
EPS = 1e-05
THETA = 10000.0
MASK_FILL = -1e30
F32 = jnp.float32
BF16 = jnp.bfloat16
NT = (((1,), (1,)), ((), ()))
CORES = 2
SWAP_ROWS = 16
MIB = 2**20


def dot(a, b):
    return jnp.dot(a, b, preferred_element_type=F32)


def dot_nt(a, b):
    return lax.dot_general(a, b, NT, preferred_element_type=F32)


def call(kernel, name, outs, args, smem=0, scratch=(), limit=32, us=10):
    specs = [pl.BlockSpec(memory_space=pltpu.SMEM)] * smem
    specs += [pl.BlockSpec(memory_space=pltpu.VMEM)] * (len(args) - smem)
    return pl.pallas_call(
        kernel,
        out_shape=tuple(jax.ShapeDtypeStruct(s, d) for s, d in outs),
        in_specs=specs,
        out_specs=tuple(pl.BlockSpec(memory_space=pltpu.VMEM) for _ in outs),
        scratch_shapes=list(scratch),
        compiler_params=pltpu.CompilerParams(vmem_limit_bytes=limit * MIB),
        cost_estimate=pl.CostEstimate(
            flops=int(us * 1e9), bytes_accessed=0, transcendentals=0
        ),
        name=name,
    )(*args)


class Plan:
    def __init__(self, nd, nc):
        self.nd, self.nz = nd, nc // CORES
        self.kd, self.kz = nd.bit_length() - 1, self.nz.bit_length() - 1
        self.core = lax.axis_index("ctx") % CORES
        self.z = lax.axis_index("ctx") // CORES
        self.d = lax.axis_index("dp")

    def order(self, k, core):
        return [(j + core) % k for j in range(k)]

    def masks(self, k, core):
        order = self.order(k, core)
        return [
            sum(1 << order[j] for j in range(k) if (p >> j) & 1) for p in range(1 << k)
        ]

    def place(self, d, z, c):
        return (d * self.nz + z) * CORES + c

    def everywhere(self):
        for d in range(self.nd):
            for z in range(self.nz):
                for c in range(CORES):
                    yield d, z, c

    def hop_d(self, x, j):
        perm = [
            (
                self.place(d, z, c),
                self.place(d ^ (1 << self.order(self.kd, c)[j]), z, c),
            )
            for d, z, c in self.everywhere()
        ]
        return lax.ppermute(x, ("dp", "ctx"), perm)

    def hop_z(self, x, j):
        perm = [
            (
                self.place(d, z, c),
                self.place(d, z ^ (1 << self.order(self.kz, c)[j]), c),
            )
            for d, z, c in self.everywhere()
        ]
        return lax.ppermute(x, ("dp", "ctx"), perm)

    def swap(self, x):
        perm = [(self.place(d, z, c), self.place(d, z, 1 - c)) for d, z, c in self.everywhere()]
        return lax.ppermute(x, ("dp", "ctx"), perm)

    def spread(self, x, k, hop):
        held = [x]
        for j in range(k):
            for h in list(held):
                held.append(hop(h, j))
                yield held[-1]
        return held

    def fold(self, parts, k, hop):
        terms = [[p] for p in parts]
        for j in reversed(range(k)):
            for p in reversed(range(1 << j, 2 << j)):
                got = hop(add(*terms[p]), j)
                terms[p - (1 << j)].append(got)
                yield got
        return add(*terms[0])

    def owners(self):
        m0 = jnp.array(self.masks(self.kd, 0), jnp.int32)
        m1 = jnp.array(self.masks(self.kd, 1), jnp.int32)
        mine = jnp.where(self.core == 0, m0, m1) ^ self.d
        other = jnp.where(self.core == 0, m1, m0) ^ self.d
        return jnp.concatenate([self.core[None], mine, other]).astype(jnp.int32)

    def total_z(self, x):
        sizes = []
        for j in reversed(range(self.kz)):
            order = jnp.where(
                self.core == 0, self.order(self.kz, 0)[j], self.order(self.kz, 1)[j]
            )
            bit = (self.z >> order) & 1
            rows = x.shape[0]
            size = -(-rows // 16) * 8
            keep = lax.dynamic_slice_in_dim(x, bit * (rows - size), size, 0)
            send = lax.dynamic_slice_in_dim(x, (1 - bit) * (rows - size), size, 0)
            sizes.append((bit, rows, size))
            got = self.hop_z(send, j)
            yield got
            x = add(keep, got)
        for j in range(self.kz):
            bit, rows, size = sizes.pop()
            got = self.hop_z(x, j)
            yield got
            low = jnp.where(bit == 0, x, got)
            high = jnp.where(bit == 0, got, x)
            x = jnp.concatenate([low[: rows - size], high], axis=0)
        return x

    def reduce_all(self, parts):
        x = yield from self.fold(parts, self.kd, self.hop_d)
        x = yield from self.total_z(x)
        other = self.swap(x)
        yield other
        return jnp.where(self.core == 0, x, other), jnp.where(self.core == 0, other, x)


class Task:
    def __init__(self, steps):
        self.steps, self.out, self.done, self.result = steps, [], False, None

    def go(self, n=1000):
        while n > 0 and not self.done:
            try:
                self.out.append(next(self.steps))
            except StopIteration as stop:
                self.done, self.result = True, stop.value
            n -= 1
        return self

    def finish(self):
        return self.go().result


def after(x, *tasks):
    waited = []
    for task in tasks:
        if isinstance(task, Task):
            waited += task.out
            task.out = []
        else:
            waited.append(task)
    return lax.optimization_barrier((x, *waited))[0] if waited else x


def add(*terms):
    if len(terms) == 1:
        return terms[0]
    return functools.reduce(lambda a, b: a + b, [t.astype(F32) for t in terms]).astype(BF16)


def row_split(rows):
    offset = rows // 2 // 16 * 16
    return offset, rows - offset


def start_row(idx, slot, parity, rows, offset):
    return pl.multiple_of(idx[slot] * rows + parity * offset, 8)


def pack_kernel(nd, idx, gate, up, down_t, first, second):
    rows = gate.shape[0]
    down = down_t[...].T
    shard = down.shape[0]
    quarter = shard // 4
    outs = (first, second)
    for core in range(CORES):

        @pl.when(idx[0] == core)
        def _(core=core):
            for f in range(2):
                at = core * 2 * quarter + f * quarter
                out = outs[f]
                for j in range(nd):
                    src = slice(j * shard + at, j * shard + at + quarter)
                    dst = slice(j * quarter, (j + 1) * quarter)
                    out[0:rows, dst] = gate[:, src]
                    out[rows : 2 * rows, dst] = up[:, src]
                width = nd * quarter
                block = down[at : at + quarter, :]
                out[2 * rows : 2 * rows + quarter, :] = block[:, :width]
                tail = 2 * rows + quarter
                half = quarter // 2
                rest = block.shape[1] - width
                out[tail : tail + half, 0:rest] = block[:half, width:]
                out[tail : tail + half, rest:] = block[half:, width:]


def gain_column(gain_ref, which):
    lane = (QW + 2 * KW) % 128 + which
    return gain_ref[...].astype(F32)[:, lane : lane + 1]


def project_kernel(nd, idx, pos, cos, sin, x_ref, *refs):
    pieces = refs[: 2 * nd]
    normed_ref, q_ref, kv_ref, w_ref, gain_ref = refs[2 * nd :]
    model = x_ref.shape[0]
    rows = model // nd
    offset, take = row_split(rows)
    core = idx[0]
    for p in range(nd):
        w_ref[pl.ds(start_row(idx, 1 + p, core, rows, offset), take), :] = pieces[p][...]
        w_ref[pl.ds(start_row(idx, 1 + nd + p, 1 - core, rows, offset), take), :] = pieces[
            nd + p
        ][...]
    low = (QW + 2 * KW) // 128 * 128
    gain_ref[...] = w_ref[:, low : low + 128]
    x = x_ref[...].astype(F32)
    factor = lax.rsqrt(jnp.mean(x * x, axis=0, keepdims=True) + EPS)
    normed = (x * factor * gain_column(gain_ref, 0)).astype(BF16)
    normed_ref[...] = normed
    normed = normed.T
    half = HEAD_SIZE // 2
    c, s = cos[...], sin[...]
    heads = 10
    for b in range(0, w_ref.shape[1], heads * HEAD_SIZE):
        block = dot(normed, w_ref[:, b : b + heads * HEAD_SIZE]).T
        for i in range(heads):
            head = b // HEAD_SIZE + i
            if head >= QUERY_HEADS + 2 * KEY_VALUE_HEADS:
                break
            u1 = block[i * HEAD_SIZE : i * HEAD_SIZE + half]
            u2 = block[i * HEAD_SIZE + half : (i + 1) * HEAD_SIZE]
            if head < QUERY_HEADS + KEY_VALUE_HEADS:
                u1, u2 = u1 * c - u2 * s, u2 * c + u1 * s
            both = jnp.concatenate([u1, u2], axis=0).astype(BF16)
            if head < QUERY_HEADS:
                q_ref[head * HEAD_SIZE : (head + 1) * HEAD_SIZE] = (
                    both.astype(F32) * HEAD_SIZE**-0.5
                ).astype(BF16)
            else:
                at = (head - QUERY_HEADS) * HEAD_SIZE
                kv_ref[at : at + HEAD_SIZE] = both
    run = x_ref.shape[1] // 2
    blocks = jnp.broadcast_to(
        (pos[...] // run).astype(F32), (kv_ref.shape[0] - 2 * KW, x_ref.shape[1])
    )
    kv_ref[2 * KW :, :] = blocks.astype(BF16)


def list_pairs(q_blocks, kv_s, count, run, todo):
    n = jnp.int32(0)
    for rank in range(count):
        for part in range(2):
            tile = kv_s[rank, 2 * KW : 2 * KW + 16, part * run : part * run + 128]
            block = jnp.max(tile.astype(F32)).astype(jnp.int32)
            for r in range(2):
                active = block < q_blocks[r]

                @pl.when(active)
                def _(n=n, code=r * 256 + rank * 2 + part):
                    todo[n] = code

                n = n + active.astype(jnp.int32)
    return n


def each_pair(todo, n, run, pair):
    def body(i, _):
        code = todo[i]
        r = code // 256
        block = code % 256
        pair(
            block // 2,
            pl.multiple_of((block % 2) * run, run),
            pl.multiple_of(r * run, run),
            False,
        )
        return 0

    lax.fori_loop(0, n, body, 0)


def forward_kernel(count, first, last, run, q_blocks, qT, *refs):
    kvs, refs = refs[:count], refs[count:]
    if not first:
        m_in, l_in, acc_in = refs[:3]
        refs = refs[3:]
    if last:
        o_ref, lse_ref, kv_s, m_s, l_s, acc_s, todo = refs
    else:
        m_s, l_s, acc_s, kv_s, todo = refs
    for i in range(count):
        kv_s[i] = kvs[i][...]
    if not first:
        m_s[...] = m_in[...]
        l_s[...] = l_in[...]
        acc_s[...] = acc_in[...]
    n = list_pairs(q_blocks, kv_s, count, run, todo)
    keep = lax.broadcasted_iota(jnp.int32, (run, run), 0) <= lax.broadcasted_iota(
        jnp.int32, (run, run), 1
    )

    def pair(rank, ko, qo, diag):
        def scores(hd):
            h = hd // GROUPS
            k = kv_s[rank, h * HEAD_SIZE : (h + 1) * HEAD_SIZE, pl.ds(ko, run)].T
            return dot(k, qT[hd * HEAD_SIZE : (hd + 1) * HEAD_SIZE, pl.ds(qo, run)])

        def flush(hd, p, shrink):
            h = KEY_VALUE_HEADS + hd // GROUPS
            vT = kv_s[rank, h * HEAD_SIZE : (h + 1) * HEAD_SIZE, pl.ds(ko, run)]
            o = dot(vT, p)
            rows = slice(hd * HEAD_SIZE, (hd + 1) * HEAD_SIZE)
            if shrink is not None:
                o = acc_s[rows, pl.ds(qo, run)] * shrink + o
            acc_s[rows, pl.ds(qo, run)] = o

        if not diag:
            m_all = m_s[:, pl.ds(qo, run)]
            l_all = l_s[:, pl.ds(qo, run)]

        def top(hd, s):
            if diag:
                s = jnp.where(keep, s, MASK_FILL)
            m = jnp.max(s, axis=0, keepdims=True)
            if not diag:
                m = jnp.maximum(m_all[hd : hd + 1], m)
            return s, m

        ms, ls, pending = [], [], None
        current = top(0, scores(0))
        following = scores(1)
        for hd in range(QUERY_HEADS):
            s, m = current
            if hd + 1 < QUERY_HEADS:
                current = top(hd + 1, following)
            if hd + 2 < QUERY_HEADS:
                following = scores(hd + 2)
            if pending is not None:
                flush(*pending)
            p = jnp.exp(s - m)
            total = jnp.sum(p, axis=0, keepdims=True)
            shrink = None
            if not diag:
                shrink = jnp.exp(m_all[hd : hd + 1] - m)
                total = l_all[hd : hd + 1] * shrink + total
            ms.append(m)
            ls.append(total)
            pending = (hd, p.astype(BF16), shrink)
        flush(*pending)
        m_s[:, pl.ds(qo, run)] = jnp.concatenate(ms + ms[-1:], 0)
        l_s[:, pl.ds(qo, run)] = jnp.concatenate(ls + ls[-1:], 0)

    if first:
        for r in range(2):
            pair(0, r * run, r * run, True)
    each_pair(todo, n, run, pair)
    if last:
        lse_ref[...] = m_s[...] + jnp.log(l_s[...])
        for hd in range(QUERY_HEADS):
            rows = slice(hd * HEAD_SIZE, (hd + 1) * HEAD_SIZE)
            o_ref[rows, :] = (acc_s[rows, :] / l_s[hd : hd + 1, :]).astype(BF16)


def forward_wave(q_blocks, qT, kvs, state, last, us):
    tokens = qT.shape[1]
    stats = pltpu.VMEM((16, tokens), F32)
    kv_s = pltpu.VMEM((len(kvs),) + kvs[0].shape, BF16)
    todo = pltpu.SMEM((4 * len(kvs),), jnp.int32)
    first = state is None
    args = [q_blocks, qT] + list(kvs) + ([] if first else list(state))
    if last:
        outs = [((QW, tokens), BF16), ((16, tokens), F32)]
        scratch = [kv_s, stats, stats, pltpu.VMEM((QW, tokens), F32), todo]
    else:
        outs = [((16, tokens), F32), ((16, tokens), F32), ((QW, tokens), F32)]
        scratch = [kv_s, todo]
    return call(
        functools.partial(forward_kernel, len(kvs), first, last, tokens // 2),
        "attention_forward",
        outs,
        args,
        smem=1,
        scratch=scratch,
        limit=24 + 2 * len(kvs),
        us=us,
    )


def backward_kernel(count, first, diag_here, run, q_blocks, qT, doT, lse, delta, *refs):
    kvs, refs = refs[:count], refs[count:]
    if not first:
        dq_in, refs = refs[0], refs[1:]
    dq_s, outs, (kv_s, dkv_s, todo) = refs[0], refs[1 : 1 + count], refs[1 + count :]
    for i in range(count):
        kv_s[i] = kvs[i][...]
    dkv_s[...] = jnp.zeros_like(dkv_s)
    dq_s[...] = jnp.zeros_like(dq_s) if first else dq_in[...]
    n = list_pairs(q_blocks, kv_s, count, run, todo)
    keep = lax.broadcasted_iota(jnp.int32, (run, run), 0) <= lax.broadcasted_iota(
        jnp.int32, (run, run), 1
    )

    def pair(rank, ko, qo, diag):
        lse_all = lse[:, pl.ds(qo, run)]
        delta_all = delta[:, pl.ds(qo, run)]

        def rows(h):
            return slice(h * HEAD_SIZE, (h + 1) * HEAD_SIZE)

        def opening(hd):
            h = hd // GROUPS
            k = kv_s[rank, rows(h), pl.ds(ko, run)].T
            v = kv_s[rank, rows(KEY_VALUE_HEADS + h), pl.ds(ko, run)].T
            return dot(k, qT[rows(hd), pl.ds(qo, run)]), dot(v, doT[rows(hd), pl.ds(qo, run)])

        def closing(hd, p, ds):
            h = hd // GROUPS
            q = qT[rows(hd), pl.ds(qo, run)]
            do = doT[rows(hd), pl.ds(qo, run)]
            kT = kv_s[rank, rows(h), pl.ds(ko, run)]
            dkv_s[rank, rows(KEY_VALUE_HEADS + h), pl.ds(ko, run)] += dot_nt(do, p)
            dkv_s[rank, rows(h), pl.ds(ko, run)] += dot_nt(q, ds)
            dq_s[rows(hd), pl.ds(qo, run)] += dot(kT, ds)

        following, pending = opening(0), None
        for hd in range(QUERY_HEADS):
            s, dp = following
            if hd + 1 < QUERY_HEADS:
                following = opening(hd + 1)
            if pending is not None:
                closing(*pending)
            p = jnp.exp(s - lse_all[hd : hd + 1])
            if diag:
                p = jnp.where(keep, p, 0.0)
            ds = (p * (dp - delta_all[hd : hd + 1])).astype(BF16)
            pending = (hd, p.astype(BF16), ds)
        closing(*pending)

    if diag_here:
        for r in range(2):
            pair(0, r * run, r * run, True)
    each_pair(todo, n, run, pair)
    for i in range(count):
        outs[i][...] = dkv_s[i].astype(BF16)


def backward_wave(q_blocks, qT, doT, lse, delta, kvs, dq, diag, us):
    tokens = qT.shape[1]
    count = len(kvs)
    args = [q_blocks, qT, doT, lse, delta] + list(kvs) + ([] if dq is None else [dq])
    got = call(
        functools.partial(backward_kernel, count, dq is None, diag, tokens // 2),
        "attention_backward",
        [((QW, tokens), F32)] + [((2 * KW, tokens), BF16)] * count,
        args,
        smem=1,
        scratch=[
            pltpu.VMEM((count,) + kvs[0].shape, BF16),
            pltpu.VMEM((count, 2 * KW, tokens), F32),
            pltpu.SMEM((4 * count,), jnp.int32),
        ],
        limit=24 + 4 * count,
        us=us,
    )
    return got[0], list(got[1:])


def middle_kernel(nd, idx, x_ref, oT, gain_ref, *refs):
    pieces = refs[: 2 * nd]
    mid_ref, normed_ref, w_ref = refs[2 * nd :]
    rows = w_ref.shape[0] // nd
    offset, take = row_split(rows)
    core = idx[0]
    for p in range(nd):
        w_ref[pl.ds(start_row(idx, 1 + p, core, rows, offset), take), :] = pieces[p][...]
        w_ref[pl.ds(start_row(idx, 1 + nd + p, 1 - core, rows, offset), take), :] = pieces[
            nd + p
        ][...]
    mid = x_ref[...].astype(F32) + dot(w_ref[...].T, oT[...])
    mid_ref[...] = mid
    factor = lax.rsqrt(jnp.mean(mid * mid, axis=0, keepdims=True) + EPS)
    normed_ref[...] = (mid * factor * gain_column(gain_ref, 1)).astype(BF16)


def mlp_kernel(nd, first, idx, n_own, n_sib, dy_own, dy_sib, *refs):
    pieces, refs = refs[:nd], refs[nd:]
    if not first:
        before, refs = refs[:4], refs[4:]
    sums, grads, refs = refs[:4], refs[4 : 4 + nd], refs[4 + nd :]
    wg, wu, wd, wgT, wuT, wdT, nT, dyT, actT, dg_s, du_s = refs
    model = wg.shape[0]
    rows, quarter, width = model // nd, wd.shape[0] // nd, wd.shape[0]
    half, rest, tail = quarter // 2, model - width, 2 * rows + quarter
    tokens = n_own.shape[1]
    for p in range(nd):
        d = idx[1 + p]
        at = pl.multiple_of(d * rows, 8)
        wg[pl.ds(at, rows), :] = pieces[p][0:rows]
        wu[pl.ds(at, rows), :] = pieces[p][rows : 2 * rows]
        at = pl.multiple_of(d * quarter, 16)
        wd[pl.ds(at, quarter), 0:width] = pieces[p][2 * rows : tail]
        wd[pl.ds(at, half), width:] = pieces[p][tail:, 0:rest]
        at = pl.multiple_of(d * quarter + half, 8)
        wd[pl.ds(at, half), width:] = pieces[p][tail:, rest:]
    wgT[...] = wg[...].T
    wuT[...] = wu[...].T
    wdT[...] = wd[...].T
    nT[:, 0:tokens] = n_own[...]
    nT[:, tokens:] = n_sib[...]
    dyT[:, 0:tokens] = dy_own[...]
    dyT[:, tokens:] = dy_sib[...]
    step = 256

    def opening(at):
        n, dy = nT[:, at : at + step], dyT[:, at : at + step]
        return dot(wgT[...], n), dot(wuT[...], n), dot(wd[...], dy)

    following = opening(0)
    for at in range(0, 2 * tokens, step):
        g, u, ga = following
        if at + step < 2 * tokens:
            following = opening(at + step)
        s = jax.nn.sigmoid(g)
        gs = g * s
        act = (gs * u).astype(BF16)
        du = (ga * gs).astype(BF16)
        dg = (ga * u * (s + gs * (1.0 - s))).astype(BF16)
        actT[:, at : at + step] = act
        dg_s[:, at : at + step] = dg
        du_s[:, at : at + step] = du
        out = dot(wdT[...], act)
        gn = dot(wg[...], dg) + dot(wu[...], du)
        r, to = at // tokens, at % tokens
        if not first:
            out = out + before[r][:, to : to + step].astype(F32)
            gn = gn + before[2 + r][:, to : to + step].astype(F32)
        sums[r][:, to : to + step] = out.astype(BF16)
        sums[2 + r][:, to : to + step] = gn.astype(BF16)
    for p in range(nd):
        d = idx[1 + p]
        n_rows = nT[pl.ds(pl.multiple_of(d * rows, 8), rows), :]
        grads[p][0:rows] = dot_nt(n_rows, dg_s[...]).astype(BF16)
        grads[p][rows : 2 * rows] = dot_nt(n_rows, du_s[...]).astype(BF16)
        a_rows = actT[pl.ds(pl.multiple_of(d * quarter, 16), quarter), :]
        down = dot_nt(a_rows, dyT[...]).astype(BF16)
        grads[p][2 * rows : tail] = down[:, :width]
        grads[p][tail:, 0:rest] = down[:half, width:]
        grads[p][tail:, rest:] = down[half:, width:]


def mlp_part(idx, nd, normed, normed_sib, dy, dy_sib, pieces, before, us):
    model, tokens = normed.shape
    size, width = pieces[0].shape
    args = [idx, normed, normed_sib, dy, dy_sib] + list(pieces) + ([] if before is None else before)
    got = call(
        functools.partial(mlp_kernel, nd, before is None),
        "mlp",
        [((model, tokens), BF16)] * 4 + [((size, width), BF16)] * nd,
        args,
        smem=1,
        scratch=[
            pltpu.VMEM((model, width), BF16),
            pltpu.VMEM((model, width), BF16),
            pltpu.VMEM((width, model), BF16),
            pltpu.VMEM((width, model), BF16),
            pltpu.VMEM((width, model), BF16),
            pltpu.VMEM((model, width), BF16),
            pltpu.VMEM((model, 2 * tokens), BF16),
            pltpu.VMEM((model, 2 * tokens), BF16),
            pltpu.VMEM((width, 2 * tokens), BF16),
            pltpu.VMEM((width, 2 * tokens), BF16),
            pltpu.VMEM((width, 2 * tokens), BF16),
        ],
        limit=48,
        us=us,
    )
    return list(got[:4]), list(got[4:])


def norm_backward(x, gain, grad):
    factor = lax.rsqrt(jnp.mean(x * x, axis=0, keepdims=True) + EPS)
    scaled = grad * gain
    along = jnp.mean(scaled * x, axis=0, keepdims=True)
    grad_x = factor * scaled - x * (factor * factor * factor * along)
    grad_gain = jnp.sum(grad * x * factor, axis=1, keepdims=True)
    return grad_x, grad_gain


def turn_kernel(idx, mid_ref, gain_ref, out_own, out_got, gn_own, gn_got, dy_ref, oT, w_ref, *refs):
    out_ref, gmid_ref, half_ref, doT, delta, column = refs
    mid = mid_ref[...]
    out_ref[...] = (mid + (out_own[...].astype(F32) + out_got[...].astype(F32))).astype(BF16)
    grad = gn_own[...].astype(F32) + gn_got[...].astype(F32)
    grad_mid, grad_gain = norm_backward(mid, gain_column(gain_ref, 1), grad)
    grad_mid = grad_mid + dy_ref[...].astype(F32)
    gmid_ref[...] = grad_mid
    half = grad_mid.astype(BF16)
    half_ref[...] = half
    heads = dot(w_ref[...], half).astype(BF16)
    doT[...] = heads
    for hd in range(QUERY_HEADS):
        rows = slice(hd * HEAD_SIZE, (hd + 1) * HEAD_SIZE)
        delta[hd : hd + 1, :] = jnp.sum(
            oT[rows, :].astype(F32) * heads[rows].astype(F32), axis=0, keepdims=True
        )
    delta[QUERY_HEADS:, :] = jnp.zeros_like(delta[QUERY_HEADS:, :])
    column[...] = jnp.broadcast_to(grad_gain, column.shape).astype(BF16)


def unrotate(head, cos, sin):
    half = HEAD_SIZE // 2
    g1, g2 = head[:half], head[half:]
    return jnp.concatenate([g1 * cos + g2 * sin, g2 * cos - g1 * sin], axis=0)


def query_kernel(nd, idx, dq, cos, sin, nT, oT, half_ref, column, gq_ref, *parts):
    c, s = cos[...], sin[...]
    for hd in range(QUERY_HEADS):
        rows = slice(hd * HEAD_SIZE, (hd + 1) * HEAD_SIZE)
        gq_ref[rows, :] = (unrotate(dq[rows, :] * HEAD_SIZE**-0.5, c, s)).astype(BF16)
    model = half_ref.shape[0]
    rows = nT.shape[0] // nd
    offset, take = row_split(rows)
    for k in range(2):
        parity = idx[0] if k == 0 else 1 - idx[0]
        for p in range(nd):
            at = pl.ds(start_row(idx, 1 + k * nd + p, parity, rows, offset), take)
            part = parts[p] if k == 0 else parts[nd].at[p * take : (p + 1) * take]
            part[:, 0:model] = dot_nt(oT[at, :], half_ref[...]).astype(BF16)
            part[:, model : model + 64] = column[at, 0:64]
            part[:, model + 64 :] = dot_nt(nT[at, :], gq_ref[...]).astype(BF16)


def last_kernel(nd, terms, idx, x_ref, gain_ref, cos, sin, nT, gq, w_ref, gmid_ref, *refs):
    dkvs, refs = refs[:terms], refs[terms:]
    gx_ref, parts, gp, column = refs[0], refs[1 : 2 + nd], refs[2 + nd], refs[3 + nd]
    gkv = gp.at[QW : QW + 2 * KW]
    gp[0:QW] = gq[...]
    gp[QW + 2 * KW :] = jnp.zeros((gp.shape[0] - QW - 2 * KW, gp.shape[1]), BF16)
    c, s = cos[...], sin[...]
    for h in range(2 * KEY_VALUE_HEADS):
        rows = slice(h * HEAD_SIZE, (h + 1) * HEAD_SIZE)
        block = functools.reduce(lambda a, b: a + b, [t[rows, :].astype(F32) for t in dkvs])
        if h < KEY_VALUE_HEADS:
            block = unrotate(block, c, s)
        gkv[rows, :] = block.astype(BF16)
    wide = dot(w_ref[...], gp[...])
    x = x_ref[...].astype(F32)
    grad_x, grad_gain = norm_backward(x, gain_column(gain_ref, 0), wide)
    gx_ref[...] = (grad_x + gmid_ref[...]).astype(BF16)
    column[...] = jnp.broadcast_to(grad_gain, column.shape).astype(BF16)
    rows = nT.shape[0] // nd
    offset, take = row_split(rows)
    for k in range(2):
        parity = idx[0] if k == 0 else 1 - idx[0]
        for p in range(nd):
            at = pl.ds(start_row(idx, 1 + k * nd + p, parity, rows, offset), take)
            part = parts[p] if k == 0 else parts[nd].at[p * take : (p + 1) * take]
            part[:, 0 : 2 * KW] = dot_nt(nT[at, :], gkv[...]).astype(BF16)
            part[:, 2 * KW :] = column[at, :]


def unpack_kernel(nd, first_0, first_1, second_0, second_1, gate, up, down_t):
    rows = gate.shape[0]
    quarter = down_t.shape[1] // 4
    width = nd * quarter
    half, rest, tail = quarter // 2, down_t.shape[0] - width, 2 * rows + quarter
    for f, pair in enumerate(((first_0, first_1), (second_0, second_1))):
        for core in range(CORES):
            pack = pair[core][...].astype(F32)
            at = core * 2 * quarter + f * quarter
            for j in range(nd):
                dst = slice(j * 4 * quarter + at, j * 4 * quarter + at + quarter)
                src = slice(j * quarter, (j + 1) * quarter)
                gate[:, dst] = pack[0:rows, src]
                up[:, dst] = pack[rows : 2 * rows, src]
            last = jnp.concatenate([pack[tail:, 0:rest], pack[tail:, rest:]], axis=0)
            block = jnp.concatenate([pack[2 * rows : tail], last], axis=1)
            down_t[:, at : at + quarter] = block.T


def local(
    nd, nc, tokens, positions, w_qkv, w_out, w_gate, w_up, w_down, g_attn, g_mlp, grad_out
):
    plan = Plan(nd, nc)
    idx = plan.owners()
    x = tokens[0].T
    dy = grad_out[0].T
    model, count = x.shape
    shard = w_qkv.shape[0]
    offset, take = row_split(shard)
    start = plan.core * offset
    run = count // 2
    width = QW + 2 * KW

    def slice_rows(a):
        return lax.dynamic_slice_in_dim(a, start, take, 0)

    pad = jnp.zeros((take, 62), BF16)
    qkv_part = jnp.concatenate(
        [slice_rows(w_qkv), slice_rows(g_attn)[:, None], slice_rows(g_mlp)[:, None], pad], axis=1
    )
    out_part = slice_rows(w_out)
    qkv_parts = Task(plan.spread(qkv_part, plan.kd, plan.hop_d)).finish()
    qkv_sib = [plan.swap(p) for p in qkv_parts]

    size = 2 * shard + w_down.shape[0] * 3 // 8
    mlp_width = w_gate.shape[1] // 4
    packs = call(
        functools.partial(pack_kernel, nd),
        "pack",
        [((size, mlp_width), BF16)] * 2,
        [idx, w_gate, w_up, w_down.T],
        smem=1,
        limit=16,
        us=4,
    )
    out_task = Task(plan.spread(after(out_part, *qkv_parts[1:]), plan.kd, plan.hop_d)).go(2)
    first_task = Task(plan.spread(after(packs[0], *qkv_parts[1:]), plan.kd, plan.hop_d)).go(1)
    second_task = Task(plan.spread(packs[1], plan.kd, plan.hop_d))
    dy_sib = plan.swap(dy)

    pos = positions[0]
    q_blocks = pos[::run] // run
    half = HEAD_SIZE // 2
    freqs = THETA ** (-(jnp.arange(half).astype(F32) * 2.0) / HEAD_SIZE)
    angles = freqs[:, None] * pos.astype(F32)[None, :]
    cos, sin = jnp.cos(angles), jnp.sin(angles)

    normed, qT, kv, w_full, gains = call(
        functools.partial(project_kernel, nd),
        "project",
        [
            ((model, count), BF16),
            ((QW, count), BF16),
            ((2 * KW + 16, count), BF16),
            ((model, width + 64), BF16),
            ((model, 128), BF16),
        ],
        [after(idx, *packs), pos[None], cos, sin, x] + qkv_parts + qkv_sib,
        smem=1,
        limit=32,
        us=6,
    )

    pieces = 1 << plan.kz
    waves = [[p] for p in range(pieces)]
    kv_own = [kv]
    kv_sib = [plan.swap(kv)]
    for j in range(plan.kz):
        kv_own.append(plan.hop_z(kv, j))
    state = forward_wave(q_blocks, qT, [kv, kv_sib[0]], None, False, 8)
    out_task.go()
    first_task.go(1)
    first_at = {1 << j: kv_own[1 + j] for j in range(plan.kz)}
    kv_own = [kv] + [first_at.get(p) for p in range(1, pieces)]
    for w in range(1, pieces):
        if kv_own[w] is None:
            j = w.bit_length() - 1
            kv_own[w] = plan.hop_z(kv_own[w - (1 << j)], j)
        if w == 1 and pieces == 4:
            kv_own[3] = plan.hop_z(after(kv_own[1], state[0]), 1)
        kv_sib.append(plan.swap(kv_own[w]))
        if w == 1:
            blocks = after(q_blocks, out_task)
        elif w == 2:
            blocks = after(q_blocks, first_task)
            first_task.go()
            second_task.go(1)
        else:
            blocks = after(q_blocks, first_task)
            second_task.go(1)
        state = forward_wave(blocks, qT, [kv_own[w], kv_sib[w]], state, w == pieces - 1, 8)
    oT, lse = state
    out_parts = out_task.finish()
    out_sib = [plan.swap(p) for p in out_parts]
    mlp_parts = [first_task.finish(), second_task.finish()]

    mid, normed_two, w_out_full = call(
        functools.partial(middle_kernel, nd),
        "middle",
        [((model, count), F32), ((model, count), BF16), ((QW, model), BF16)],
        [idx, x, oT, gains] + out_parts + out_sib,
        smem=1,
        limit=24,
        us=5,
    )
    normed_two_sib = plan.swap(normed_two)
    sums, grads = mlp_part(
        idx, nd, normed_two, normed_two_sib, dy, dy_sib, mlp_parts[0], None, 14
    )
    first_total = Task(plan.reduce_all(grads)).go(2)
    sums, grads = mlp_part(
        idx, nd, normed_two, normed_two_sib, dy, dy_sib, mlp_parts[1], sums, 14
    )
    second_total = Task(plan.reduce_all(grads))
    gn_got = plan.swap(sums[3])
    out_got = plan.swap(sums[1])
    turn_idx = after(idx, first_total)
    first_total.go(1)
    output, grad_mid, grad_half, doT, delta, column = call(
        turn_kernel,
        "turn",
        [
            ((model, count), BF16),
            ((model, count), F32),
            ((model, count), BF16),
            ((QW, count), BF16),
            ((16, count), F32),
            ((model, 128), BF16),
        ],
        [turn_idx, mid, gains, sums[0], out_got, sums[2], gn_got, dy, oT, w_out_full],
        smem=1,
        limit=40,
        us=8,
    )

    totals = [None] * pieces
    back = [[3], [1, 2], [0]] if plan.kz == 2 else [[p] for p in reversed(range(pieces))]
    dq = None

    def backward(wave, blocks):
        kvs = [kv_own[p] for p in wave] + [kv_sib[p] for p in wave]
        new_dq, dkv = backward_wave(
            blocks, qT, doT, lse, delta, kvs, dq, 0 in wave, 10 * len(wave)
        )
        for i, p in enumerate(wave):
            totals[p] = [dkv[i], plan.swap(dkv[len(wave) + i])]
        return new_dq

    blocks = after(q_blocks, first_total)
    first_total.go(1)
    second_total.go(2)
    dq = backward(back[0], blocks)
    kv_hops = []
    for w in range(1, len(back)):
        for p in back[w - 1]:
            j = p.bit_length() - 1
            got = plan.hop_z(add(*totals[p]), j)
            totals[p - (1 << j)] = (totals[p - (1 << j)] or []) + [got]
            kv_hops.append(got)
        blocks = after(q_blocks, first_total)
        first_total.go(1)
        if w == 2:
            blocks = after(blocks, second_total)
            second_total.go(1)
        kept = {p: totals[p] for p in back[w]}
        dq = backward(back[w], blocks)
        for p, terms in kept.items():
            totals[p] = totals[p] + (terms or [])

    query_idx = after(idx, first_total, second_total)
    first_total.go(1)
    second_total.go(1)
    got = call(
        functools.partial(query_kernel, nd),
        "query",
        [((QW, count), BF16)]
        + [((take, model + 64 + QW), BF16)] * nd
        + [((nd * take, model + 64 + QW), BF16)],
        [query_idx, dq, cos, sin, normed, oT, grad_half, column],
        smem=1,
        limit=40,
        us=4,
    )
    gq = got[0]

    def both_cores(parts, stacked):
        other = plan.swap(stacked)
        return [add(parts[p], other[p * take : (p + 1) * take]) for p in range(nd)]

    query_total = Task(plan.reduce_all(both_cores(got[1 : 1 + nd], got[1 + nd]))).go(2)
    terms = totals[0]
    got = call(
        functools.partial(last_kernel, nd, len(terms)),
        "last",
        [((model, count), BF16)]
        + [((take, 2 * KW + 128), BF16)] * nd
        + [((nd * take, 2 * KW + 128), BF16)],
        [after(idx, first_total, second_total, query_total), x, gains, cos, sin, normed]
        + [gq, w_full, grad_mid]
        + terms,
        smem=1,
        scratch=[pltpu.VMEM((width + 64, count), BF16), pltpu.VMEM((model, 128), BF16)],
        limit=40,
        us=6,
    )
    grad_tokens = got[0]
    kv_total = Task(plan.reduce_all(both_cores(got[1 : 1 + nd], got[1 + nd])))
    kv_halves = kv_total.finish()
    query_halves = query_total.finish()
    gate, up, down = call(
        functools.partial(unpack_kernel, nd),
        "unpack",
        [(w.shape, F32) for w in (w_gate, w_up, w_down.T)],
        list(first_total.finish()) + list(second_total.finish()),
        limit=32,
        us=6,
    )

    def whole(halves):
        low, high = halves
        return jnp.concatenate([low, high[2 * take - shard :]], axis=0).astype(F32)

    query_whole = whole(query_halves)
    kv_whole = whole(kv_halves)
    qkv_whole = jnp.concatenate([query_whole[:, model + 64 :], kv_whole[:, : 2 * KW]], axis=1)
    return (
        output.T[None],
        grad_tokens.T[None],
        qkv_whole,
        query_whole[:, :model],
        gate,
        up,
        down.T,
        kv_whole[:, 2 * KW],
        query_whole[:, model],
    )


def solution(mesh):
    rows = P("dp", None)
    stored = P("dp", "ctx", None)
    vector = P("dp")
    return jax.shard_map(
        functools.partial(local, mesh.shape["dp"], mesh.shape["ctx"]),
        mesh=mesh,
        in_specs=(stored, P("dp", "ctx"), rows, rows, rows, rows, rows, vector, vector, stored),
        out_specs=(stored, stored, rows, rows, rows, rows, rows, vector, vector),
        check_vma=False,
    )
```

```python
import functools

import jax
import jax.numpy as jnp
from jax import lax
from jax.experimental import pallas as pl
from jax.experimental.pallas import tpu as pltpu
from jax.sharding import PartitionSpec as P

QUERY_HEADS = 15
KEY_VALUE_HEADS = 5
HEAD_SIZE = 64
GROUPS = QUERY_HEADS // KEY_VALUE_HEADS
QW = QUERY_HEADS * HEAD_SIZE
KW = KEY_VALUE_HEADS * HEAD_SIZE
EPS = 1e-05
THETA = 10000.0
MASK_FILL = -1e30
F32 = jnp.float32
BF16 = jnp.bfloat16
NT = (((1,), (1,)), ((), ()))
CORES = 2
SWAP_ROWS = 16
MIB = 2**20


def dot(a, b):
    return jnp.dot(a, b, preferred_element_type=F32)


def dot_nt(a, b):
    return lax.dot_general(a, b, NT, preferred_element_type=F32)


def call(kernel, name, outs, args, smem=0, scratch=(), limit=32, us=10, aliases=None):
    specs = [pl.BlockSpec(memory_space=pltpu.SMEM)] * smem
    specs += [pl.BlockSpec(memory_space=pltpu.VMEM)] * (len(args) - smem)
    return pl.pallas_call(
        kernel,
        out_shape=tuple(jax.ShapeDtypeStruct(s, d) for s, d in outs),
        in_specs=specs,
        out_specs=tuple(pl.BlockSpec(memory_space=pltpu.VMEM) for _ in outs),
        scratch_shapes=list(scratch),
        compiler_params=pltpu.CompilerParams(vmem_limit_bytes=limit * MIB),
        cost_estimate=pl.CostEstimate(
            flops=int(us * 1e7), bytes_accessed=0, transcendentals=0
        ),
        input_output_aliases=aliases or {},
        name=name,
    )(*args)


class Plan:
    def __init__(self, nd, nc):
        self.nd, self.nz = nd, nc // CORES
        self.kd, self.kz = nd.bit_length() - 1, self.nz.bit_length() - 1
        self.core = lax.axis_index("ctx") % CORES
        self.z = lax.axis_index("ctx") // CORES
        self.d = lax.axis_index("dp")
        self.gates = ()

    def order(self, k, core):
        return [(j + core) % k for j in range(k)]

    def masks(self, k, core):
        order = self.order(k, core)
        return [
            sum(1 << order[j] for j in range(k) if (p >> j) & 1) for p in range(1 << k)
        ]

    def place(self, d, z, c):
        return (d * self.nz + z) * CORES + c

    def everywhere(self):
        for d in range(self.nd):
            for z in range(self.nz):
                for c in range(CORES):
                    yield d, z, c

    def hop_d(self, x, j):
        perm = [
            (
                self.place(d, z, c),
                self.place(d ^ (1 << self.order(self.kd, c)[j]), z, c),
            )
            for d, z, c in self.everywhere()
        ]
        return lax.ppermute(after(x, *self.gates), ("dp", "ctx"), perm)

    def hop_z(self, x, j):
        perm = [
            (
                self.place(d, z, c),
                self.place(d, z ^ (1 << self.order(self.kz, c)[j]), c),
            )
            for d, z, c in self.everywhere()
        ]
        return lax.ppermute(after(x, *self.gates), ("dp", "ctx"), perm)

    def swap(self, x):
        perm = [(self.place(d, z, c), self.place(d, z, 1 - c)) for d, z, c in self.everywhere()]
        return lax.ppermute(after(x, *self.gates), ("dp", "ctx"), perm)

    def spread(self, x, k, hop):
        held = [x]
        for j in range(k):
            for h in list(held):
                held.append(hop(h, j))
                yield held[-1]
        return held

    def fold(self, near, far, k, hop):
        terms = [near]
        for j in reversed(range(k)):
            got = hop(far, j)
            yield got
            got = after(got, *self.gates)
            terms.append(got)
            if j:
                half = got.shape[0] // 2
                far = add(*[t[half:] for t in terms])
                terms = [t[:half] for t in terms]
        return add(*terms)

    def double_z(self, x):
        for j in range(self.kz):
            got = self.hop_z(x, j)
            yield got
            x = add(x, got)
        return x

    def owners(self):
        m0 = jnp.array(self.masks(self.kd, 0), jnp.int32)
        m1 = jnp.array(self.masks(self.kd, 1), jnp.int32)
        mine = jnp.where(self.core == 0, m0, m1) ^ self.d
        other = jnp.where(self.core == 0, m1, m0) ^ self.d
        return jnp.concatenate([self.core[None], mine, other]).astype(jnp.int32)

    def total_z(self, x):
        sizes = []
        for j in reversed(range(self.kz)):
            order = jnp.where(
                self.core == 0, self.order(self.kz, 0)[j], self.order(self.kz, 1)[j]
            )
            bit = (self.z >> order) & 1
            rows = x.shape[0]
            size = -(-rows // 16) * 8
            keep = lax.dynamic_slice_in_dim(x, bit * (rows - size), size, 0)
            send = lax.dynamic_slice_in_dim(x, (1 - bit) * (rows - size), size, 0)
            sizes.append((bit, rows, size))
            got = self.hop_z(send, j)
            yield got
            got = after(got, *self.gates)
            x = add(keep, got)
        for j in range(self.kz):
            bit, rows, size = sizes.pop()
            got = self.hop_z(x, j)
            yield got
            low = jnp.where(bit == 0, x, got)
            high = jnp.where(bit == 0, got, x)
            x = jnp.concatenate([low[: rows - size], high], axis=0)
        return x

    def reduce_all(self, near, far, small=False):
        x = yield from self.fold(near, far, self.kd, self.hop_d)
        x = yield from (self.double_z if small else self.total_z)(x)
        other = self.swap(x)
        yield other
        return jnp.where(self.core == 0, x, other), jnp.where(self.core == 0, other, x)


class Task:
    def __init__(self, steps):
        self.steps, self.out, self.done, self.result = steps, [], False, None

    def go(self, n=1000):
        while n > 0 and not self.done:
            try:
                self.out.append(next(self.steps))
            except StopIteration as stop:
                self.done, self.result = True, stop.value
            n -= 1
        return self

    def finish(self):
        return self.go().result


def settle(outs, *tasks):
    waited = []
    for task in tasks:
        if isinstance(task, Task):
            waited += task.out
            task.out = []
        else:
            waited.append(task)
    if not waited:
        return tuple(outs)
    return lax.optimization_barrier((*outs, *waited))[: len(outs)]


def after(x, *tasks):
    return settle((x,), *tasks)[0]


def add(*terms):
    if len(terms) == 1:
        return terms[0]
    return functools.reduce(lambda a, b: a + b, [t.astype(F32) for t in terms]).astype(BF16)


def row_split(rows):
    offset = rows // 2 // 16 * 16
    return offset, rows - offset


def start_row(idx, slot, parity, rows, offset):
    return pl.multiple_of(idx[slot] * rows + parity * offset, 8)


def pack_kernel(nd, idx, gate, up, down_t, w_out, pack):
    rows, width = gate.shape[0], pack.shape[1]
    down = down_t[...].T
    shard, model = down.shape
    quarter = shard // 4
    rest, half = model - width, quarter // 2
    for core in range(CORES):

        @pl.when(idx[0] == core)
        def _(core=core):
            for f in range(2):
                at = core * 2 * quarter + f * quarter
                out = pack.at[pl.ds(f * (2 * rows + quarter + half), 2 * rows + quarter + half)]
                for j in range(nd):
                    src = slice(j * shard + at, j * shard + at + quarter)
                    dst = slice(j * quarter, (j + 1) * quarter)
                    out[0:rows, dst] = gate[:, src]
                    out[rows : 2 * rows, dst] = up[:, src]
                block = down[at : at + quarter, :]
                tail = 2 * rows + quarter
                out[2 * rows : tail, :] = block[:, :width]
                out[tail : tail + half, 0:rest] = block[:half, width:]
                out[tail : tail + half, rest:] = block[half:, width:]

    end = pack.shape[0] - rows - rows // 2
    half = rows // 2
    pack[end : end + rows, :] = w_out[:, :width]
    pack[end + rows :, 0:rest] = w_out[0:half, width:]
    pack[end + rows :, rest:] = w_out[half:, width:]


def gain_column(gain_ref, which):
    lane = (QW + 2 * KW) % 128 + which
    return gain_ref[...].astype(F32)[:, lane : lane + 1]


def project_kernel(nd, idx, pos, cos, sin, x_ref, *refs):
    pieces = refs[: 2 * nd]
    normed_ref, q_ref, kv_ref, w_ref, gain_ref = refs[2 * nd :]
    model = x_ref.shape[0]
    rows = model // nd
    offset, take = row_split(rows)
    core = idx[0]
    for p in range(nd):
        w_ref[pl.ds(start_row(idx, 1 + p, core, rows, offset), take), :] = pieces[p][...]
        w_ref[pl.ds(start_row(idx, 1 + nd + p, 1 - core, rows, offset), take), :] = pieces[
            nd + p
        ][...]
    low = (QW + 2 * KW) // 128 * 128
    gain_ref[...] = w_ref[:, low : low + 128]
    x = x_ref[...].astype(F32)
    factor = lax.rsqrt(jnp.mean(x * x, axis=0, keepdims=True) + EPS)
    normed = (x * factor * gain_column(gain_ref, 0)).astype(BF16)
    normed_ref[...] = normed
    normed = normed.T
    half = HEAD_SIZE // 2
    c, s = cos[...], sin[...]
    heads = 10
    for b in range(0, w_ref.shape[1], heads * HEAD_SIZE):
        block = dot(normed, w_ref[:, b : b + heads * HEAD_SIZE]).T
        for i in range(heads):
            head = b // HEAD_SIZE + i
            if head >= QUERY_HEADS + 2 * KEY_VALUE_HEADS:
                break
            u1 = block[i * HEAD_SIZE : i * HEAD_SIZE + half]
            u2 = block[i * HEAD_SIZE + half : (i + 1) * HEAD_SIZE]
            if head < QUERY_HEADS + KEY_VALUE_HEADS:
                u1, u2 = u1 * c - u2 * s, u2 * c + u1 * s
            both = jnp.concatenate([u1, u2], axis=0).astype(BF16)
            if head < QUERY_HEADS:
                q_ref[head * HEAD_SIZE : (head + 1) * HEAD_SIZE] = (
                    both.astype(F32) * HEAD_SIZE**-0.5
                ).astype(BF16)
            else:
                at = (head - QUERY_HEADS) * HEAD_SIZE
                kv_ref[at : at + HEAD_SIZE] = both
    run = x_ref.shape[1] // 2
    blocks = jnp.broadcast_to(
        (pos[...] // run).astype(F32), (kv_ref.shape[0] - 2 * KW, x_ref.shape[1])
    )
    kv_ref[2 * KW :, :] = blocks.astype(BF16)


def list_pairs(q_blocks, kv_s, count, run, todo):
    n = jnp.int32(0)
    for rank in range(count):
        for part in range(2):
            tile = kv_s[rank, 2 * KW : 2 * KW + 16, part * run : part * run + 128]
            block = jnp.max(tile.astype(F32)).astype(jnp.int32)
            for r in range(2):
                active = block < q_blocks[r]

                @pl.when(active)
                def _(n=n, code=r * 256 + rank * 2 + part):
                    todo[n] = code

                n = n + active.astype(jnp.int32)
    return n


def each_pair(todo, n, run, pair):
    def body(i, _):
        code = todo[i]
        r = code // 256
        block = code % 256
        pair(
            block // 2,
            pl.multiple_of((block % 2) * run, run),
            pl.multiple_of(r * run, run),
            False,
        )
        return 0

    lax.fori_loop(0, n, body, 0)


def forward_kernel(count, first, last, run, q_blocks, qT, *refs):
    kvs, refs = refs[:count], refs[count:]
    if not first:
        m_in, l_in, acc_in = refs[:3]
        refs = refs[3:]
    if last:
        o_ref, lse_ref, kv_s, m_s, l_s, acc_s, todo = refs
    else:
        m_s, l_s, acc_s, kv_s, todo = refs
    for i in range(count):
        kv_s[i] = kvs[i][...]
    if not first:
        m_s[...] = m_in[...]
        l_s[...] = l_in[...]
        acc_s[...] = acc_in[...]
    n = list_pairs(q_blocks, kv_s, count, run, todo)
    keep = lax.broadcasted_iota(jnp.int32, (run, run), 0) <= lax.broadcasted_iota(
        jnp.int32, (run, run), 1
    )

    def pair(rank, ko, qo, diag):
        def scores(hd):
            h = hd // GROUPS
            k = kv_s[rank, h * HEAD_SIZE : (h + 1) * HEAD_SIZE, pl.ds(ko, run)].T
            return dot(k, qT[hd * HEAD_SIZE : (hd + 1) * HEAD_SIZE, pl.ds(qo, run)])

        def flush(hd, p, shrink):
            h = KEY_VALUE_HEADS + hd // GROUPS
            vT = kv_s[rank, h * HEAD_SIZE : (h + 1) * HEAD_SIZE, pl.ds(ko, run)]
            o = dot(vT, p)
            rows = slice(hd * HEAD_SIZE, (hd + 1) * HEAD_SIZE)
            if shrink is not None:
                o = acc_s[rows, pl.ds(qo, run)] * shrink + o
            acc_s[rows, pl.ds(qo, run)] = o

        if not diag:
            m_all = m_s[:, pl.ds(qo, run)]
            l_all = l_s[:, pl.ds(qo, run)]

        def top(hd, s):
            if diag:
                s = jnp.where(keep, s, MASK_FILL)
            m = jnp.max(s, axis=0, keepdims=True)
            if not diag:
                m = jnp.maximum(m_all[hd : hd + 1], m)
            return s, m

        ms, ls, pending = [], [], None
        current = top(0, scores(0))
        following = scores(1)
        for hd in range(QUERY_HEADS):
            s, m = current
            if hd + 1 < QUERY_HEADS:
                current = top(hd + 1, following)
            if hd + 2 < QUERY_HEADS:
                following = scores(hd + 2)
            if pending is not None:
                flush(*pending)
            p = jnp.exp(s - m)
            total = jnp.sum(p, axis=0, keepdims=True)
            shrink = None
            if not diag:
                shrink = jnp.exp(m_all[hd : hd + 1] - m)
                total = l_all[hd : hd + 1] * shrink + total
            ms.append(m)
            ls.append(total)
            pending = (hd, p.astype(BF16), shrink)
        flush(*pending)
        m_s[:, pl.ds(qo, run)] = jnp.concatenate(ms + ms[-1:], 0)
        l_s[:, pl.ds(qo, run)] = jnp.concatenate(ls + ls[-1:], 0)

    if first:
        for r in range(2):
            pair(0, r * run, r * run, True)
    each_pair(todo, n, run, pair)
    if last:
        lse_ref[...] = m_s[...] + jnp.log(l_s[...])
        for hd in range(QUERY_HEADS):
            rows = slice(hd * HEAD_SIZE, (hd + 1) * HEAD_SIZE)
            o_ref[rows, :] = (acc_s[rows, :] / l_s[hd : hd + 1, :]).astype(BF16)


def forward_wave(q_blocks, qT, kvs, state, last, us):
    tokens = qT.shape[1]
    stats = pltpu.VMEM((16, tokens), F32)
    kv_s = pltpu.VMEM((len(kvs),) + kvs[0].shape, BF16)
    todo = pltpu.SMEM((4 * len(kvs),), jnp.int32)
    first = state is None
    args = [q_blocks, qT] + list(kvs) + ([] if first else list(state))
    if last:
        outs = [((QW, tokens), BF16), ((16, tokens), F32)]
        scratch = [kv_s, stats, stats, pltpu.VMEM((QW, tokens), F32), todo]
    else:
        outs = [((16, tokens), F32), ((16, tokens), F32), ((QW, tokens), F32)]
        scratch = [kv_s, todo]
    return call(
        functools.partial(forward_kernel, len(kvs), first, last, tokens // 2),
        "attention_forward",
        outs,
        args,
        smem=1,
        scratch=scratch,
        limit=12 + 2 * len(kvs),
        us=us,
    )


def backward_kernel(first, last, terms, run, q_blocks, *refs):
    q_own, q_sib, do_own, do_sib, st_own, st_sib, kv = refs[:7]
    before, refs = refs[7 : 7 + terms], refs[7 + terms :]
    if not first:
        dq_in, refs = refs[0], refs[1:]
    if last:
        dq_own, dq_sib, out, dq_s, q_s, do_s, st_s, dkv_s, todo = refs
    else:
        dq_s, out, q_s, do_s, st_s, dkv_s, todo = refs
    for s, (q, do, st) in enumerate(((q_own, do_own, st_own), (q_sib, do_sib, st_sib))):
        q_s[s] = q[...]
        do_s[s] = do[...]
        st_s[s] = st[...]
    if terms:
        dkv_s[...] = functools.reduce(lambda a, b: a + b, [t[...].astype(F32) for t in before])
    else:
        dkv_s[...] = jnp.zeros_like(dkv_s)
    dq_s[...] = jnp.zeros_like(dq_s) if first else dq_in[...]
    n = jnp.int32(0)
    for part in range(2):
        tile = kv[2 * KW : 2 * KW + 16, part * run : part * run + 128]
        block = jnp.max(tile.astype(F32)).astype(jnp.int32)
        for r in range(4):
            active = block < q_blocks[r]

            @pl.when(active)
            def _(n=n, code=r * 2 + part):
                todo[n] = code

            n = n + active.astype(jnp.int32)
    keep = lax.broadcasted_iota(jnp.int32, (run, run), 0) <= lax.broadcasted_iota(
        jnp.int32, (run, run), 1
    )

    def pair(who, ko, qo, diag):
        lse_all = st_s[who, 0:16, pl.ds(qo, run)]
        delta_all = st_s[who, 16:32, pl.ds(qo, run)]

        def rows(h):
            return slice(h * HEAD_SIZE, (h + 1) * HEAD_SIZE)

        def opening(hd):
            h = hd // GROUPS
            k = kv[rows(h), pl.ds(ko, run)].T
            v = kv[rows(KEY_VALUE_HEADS + h), pl.ds(ko, run)].T
            return (
                dot(k, q_s[who, rows(hd), pl.ds(qo, run)]),
                dot(v, do_s[who, rows(hd), pl.ds(qo, run)]),
            )

        def closing(hd, p, ds):
            h = hd // GROUPS
            q = q_s[who, rows(hd), pl.ds(qo, run)]
            do = do_s[who, rows(hd), pl.ds(qo, run)]
            kT = kv[rows(h), pl.ds(ko, run)]
            dkv_s[rows(KEY_VALUE_HEADS + h), pl.ds(ko, run)] += dot_nt(do, p)
            dkv_s[rows(h), pl.ds(ko, run)] += dot_nt(q, ds)
            dq_s[who, rows(hd), pl.ds(qo, run)] += dot(kT, ds)

        following, pending = opening(0), None
        for hd in range(QUERY_HEADS):
            s, dp = following
            if hd + 1 < QUERY_HEADS:
                following = opening(hd + 1)
            if pending is not None:
                closing(*pending)
            p = jnp.exp(s - lse_all[hd : hd + 1])
            if diag:
                p = jnp.where(keep, p, 0.0)
            ds = (p * (dp - delta_all[hd : hd + 1])).astype(BF16)
            pending = (hd, p.astype(BF16), ds)
        closing(*pending)

    if last:
        for r in range(2):
            pair(0, r * run, r * run, True)

    def body(i, _):
        code = todo[i]
        r = code // 2
        pair(
            r // 2,
            pl.multiple_of((code % 2) * run, run),
            pl.multiple_of((r % 2) * run, run),
            False,
        )
        return 0

    lax.fori_loop(0, n, body, 0)
    out[...] = dkv_s[...].astype(BF16)
    if last:
        dq_own[...] = dq_s[0]
        dq_sib[...] = dq_s[1].astype(BF16)


def backward_wave(q_blocks, qs, dos, stats, kv, before, dq, last, us):
    tokens = kv.shape[1]
    both = (2, QW, tokens)
    args = [q_blocks, *qs, *dos, *stats, kv, *before] + ([] if dq is None else [dq])
    scratch = [
        pltpu.VMEM(both, BF16),
        pltpu.VMEM(both, BF16),
        pltpu.VMEM((2, 32, tokens), F32),
        pltpu.VMEM((2 * KW, tokens), F32),
        pltpu.SMEM((16,), jnp.int32),
    ]
    out = ((2 * KW, tokens), BF16)
    if last:
        outs = [((QW, tokens), F32), ((QW, tokens), BF16), out]
        scratch = [pltpu.VMEM(both, F32)] + scratch
    else:
        outs = [(both, F32), out]
    return call(
        functools.partial(backward_kernel, dq is None, last, len(before), tokens // 2),
        "attention_backward",
        outs,
        args,
        smem=1,
        scratch=scratch,
        limit=28,
        us=us,
    )


def middle_kernel(nd, idx, x_ref, oT, gain_ref, *refs):
    pieces = refs[:nd]
    mid_ref, normed_ref, w_ref = refs[nd:]
    rows, width = w_ref.shape[0] // nd, pieces[0].shape[1]
    rest, half = w_ref.shape[1] - width, rows // 2
    end = pieces[0].shape[0] - rows - half
    for p in range(nd):
        at = pl.multiple_of(idx[1 + p] * rows, 8)
        w_ref[pl.ds(at, rows), 0:width] = pieces[p][end : end + rows]
        w_ref[pl.ds(at, half), width:] = pieces[p][end + rows :, 0:rest]
        w_ref[pl.ds(pl.multiple_of(at + half, 8), half), width:] = pieces[p][end + rows :, rest:]
    mid = x_ref[...].astype(F32) + dot(w_ref[...].T, oT[...])
    mid_ref[...] = mid
    factor = lax.rsqrt(jnp.mean(mid * mid, axis=0, keepdims=True) + EPS)
    normed_ref[...] = (mid * factor * gain_column(gain_ref, 1)).astype(BF16)


def mlp_kernel(nd, idx, n_own, n_sib, dy_own, dy_sib, *refs):
    pieces, sums, stacks = refs[:nd], refs[nd : nd + 4], refs[nd + 4 : nd + 6]
    wg, wu, wd, wgT, wuT, wdT, nT, dyT, actT, dg_s, du_s = refs[nd + 6 :]
    model = wg.shape[0]
    rows, quarter, width = model // nd, wd.shape[0] // nd, wd.shape[0]
    half, rest, tail = quarter // 2, model - width, 2 * rows + quarter
    size = tail + half
    tokens = n_own.shape[1]
    nT[:, 0:tokens] = n_own[...]
    nT[:, tokens:] = n_sib[...]
    dyT[:, 0:tokens] = dy_own[...]
    dyT[:, tokens:] = dy_sib[...]
    step = 256
    for f in range(2):
        for p in range(nd):
            d = idx[1 + p]
            piece = pieces[p].at[pl.ds(f * size, size)]
            at = pl.multiple_of(d * rows, 8)
            wg[pl.ds(at, rows), :] = piece[0:rows]
            wu[pl.ds(at, rows), :] = piece[rows : 2 * rows]
            at = pl.multiple_of(d * quarter, 16)
            wd[pl.ds(at, quarter), 0:width] = piece[2 * rows : tail]
            wd[pl.ds(at, half), width:] = piece[tail:size, 0:rest]
            at = pl.multiple_of(d * quarter + half, 8)
            wd[pl.ds(at, half), width:] = piece[tail:size, rest:]
        wgT[...] = wg[...].T
        wuT[...] = wu[...].T
        wdT[...] = wd[...].T

        def opening(at):
            n, dy = nT[:, at : at + step], dyT[:, at : at + step]
            return dot(wgT[...], n), dot(wuT[...], n), dot(wd[...], dy)

        following = opening(0)
        for at in range(0, 2 * tokens, step):
            g, u, ga = following
            if at + step < 2 * tokens:
                following = opening(at + step)
            s = jax.nn.sigmoid(g)
            gs = g * s
            act = (gs * u).astype(BF16)
            du = (ga * gs).astype(BF16)
            dg = (ga * u * (s + gs * (1.0 - s))).astype(BF16)
            actT[:, at : at + step] = act
            dg_s[:, at : at + step] = dg
            du_s[:, at : at + step] = du
            out = dot(wdT[...], act)
            gn = dot(wg[...], dg) + dot(wu[...], du)
            r, to = at // tokens, at % tokens
            if f:
                out = out + sums[r][:, to : to + step].astype(F32)
                gn = gn + sums[2 + r][:, to : to + step].astype(F32)
            sums[r][:, to : to + step] = out.astype(BF16)
            sums[2 + r][:, to : to + step] = gn.astype(BF16)
        wg[...] = dot_nt(nT[...], dg_s[...]).astype(BF16)
        wu[...] = dot_nt(nT[...], du_s[...]).astype(BF16)
        wd[...] = dot_nt(actT[...], dyT[...]).astype(BF16)
        for p in range(nd):
            d = idx[1 + p]
            grads = stacks[p // (nd // 2)].at[pl.ds((p % (nd // 2) * 2 + f) * size, size)]
            at = pl.multiple_of(d * rows, 8)
            grads[0:rows] = wg[pl.ds(at, rows), :]
            grads[rows : 2 * rows] = wu[pl.ds(at, rows), :]
            at = pl.multiple_of(d * quarter, 16)
            grads[2 * rows : tail] = wd[pl.ds(at, quarter), 0:width]
            grads[tail:, 0:rest] = wd[pl.ds(at, half), width:]
            at = pl.multiple_of(d * quarter + half, 8)
            grads[tail:, rest:] = wd[pl.ds(at, half), width:]


def norm_backward(x, gain, grad):
    factor = lax.rsqrt(jnp.mean(x * x, axis=0, keepdims=True) + EPS)
    scaled = grad * gain
    along = jnp.mean(scaled * x, axis=0, keepdims=True)
    grad_x = factor * scaled - x * (factor * factor * factor * along)
    grad_gain = jnp.sum(grad * x * factor, axis=1, keepdims=True)
    return grad_x, grad_gain


def turn_kernel(
    idx, mid_ref, gain_ref, gn_own, gn_got, dy_ref, oT, lse, w_ref, *refs
):
    gmid_ref, half_ref, doT, stats, column = refs
    stats[0:16, :] = lse[...]
    delta = stats.at[16:32]
    mid = mid_ref[...]
    grad = gn_own[...].astype(F32) + gn_got[...].astype(F32)
    grad_mid, grad_gain = norm_backward(mid, gain_column(gain_ref, 1), grad)
    grad_mid = grad_mid + dy_ref[...].astype(F32)
    gmid_ref[...] = grad_mid
    half = grad_mid.astype(BF16)
    half_ref[...] = half
    heads = dot(w_ref[...], half).astype(BF16)
    doT[...] = heads
    for hd in range(QUERY_HEADS):
        rows = slice(hd * HEAD_SIZE, (hd + 1) * HEAD_SIZE)
        delta[hd : hd + 1, :] = jnp.sum(
            oT[rows, :].astype(F32) * heads[rows].astype(F32), axis=0, keepdims=True
        )
    delta[QUERY_HEADS:, :] = jnp.zeros_like(delta[QUERY_HEADS:, :])
    column[...] = jnp.broadcast_to(grad_gain, column.shape).astype(BF16)


def unrotate(head, cos, sin):
    half = HEAD_SIZE // 2
    g1, g2 = head[:half], head[half:]
    return jnp.concatenate([g1 * cos + g2 * sin, g2 * cos - g1 * sin], axis=0)


def query_kernel(nd, idx, dq, dq_got, cos, sin, nT, oT, half_ref, column, gq_ref, *parts):
    c, s = cos[...], sin[...]
    for hd in range(QUERY_HEADS):
        rows = slice(hd * HEAD_SIZE, (hd + 1) * HEAD_SIZE)
        gq_ref[rows, :] = unrotate(
            (dq[rows, :] + dq_got[rows, :].astype(F32)) * HEAD_SIZE**-0.5, c, s
        ).astype(BF16)
    model = half_ref.shape[0]
    rows = nT.shape[0] // nd
    offset, take = row_split(rows)
    for k in range(2):
        parity = idx[0] if k == 0 else 1 - idx[0]
        for p in range(nd):
            at = pl.ds(start_row(idx, 1 + k * nd + p, parity, rows, offset), take)
            part = parts[k].at[p * take : (p + 1) * take]
            part[:, 0:model] = dot_nt(oT[at, :], half_ref[...]).astype(BF16)
            part[:, model : model + 128] = column[at, :]
            part[:, model + 128 : 2 * model + 128] = dot_nt(nT[at, :], gq_ref[...]).astype(BF16)


def last_kernel(nd, terms, idx, x_ref, gain_ref, cos, sin, nT, gq, w_ref, gmid_ref, *refs):
    dkvs, refs = refs[:terms], refs[terms:]
    gx_ref, parts, gp, column = refs[0], refs[1:3], refs[3], refs[4]
    gkv = gp.at[QW : QW + 2 * KW]
    gp[0:QW] = gq[...]
    gp[QW + 2 * KW :] = jnp.zeros((gp.shape[0] - QW - 2 * KW, gp.shape[1]), BF16)
    c, s = cos[...], sin[...]
    for h in range(2 * KEY_VALUE_HEADS):
        rows = slice(h * HEAD_SIZE, (h + 1) * HEAD_SIZE)
        block = functools.reduce(lambda a, b: a + b, [t[rows, :].astype(F32) for t in dkvs])
        if h < KEY_VALUE_HEADS:
            block = unrotate(block, c, s)
        gkv[rows, :] = block.astype(BF16)
    wide = dot(w_ref[...], gp[...])
    x = x_ref[...].astype(F32)
    grad_x, grad_gain = norm_backward(x, gain_column(gain_ref, 0), wide)
    gx_ref[...] = (grad_x + gmid_ref[...]).astype(BF16)
    column[...] = jnp.broadcast_to(grad_gain, column.shape).astype(BF16)
    rows = nT.shape[0] // nd
    offset, take = row_split(rows)
    for k in range(2):
        parity = idx[0] if k == 0 else 1 - idx[0]
        for p in range(nd):
            at = pl.ds(start_row(idx, 1 + k * nd + p, parity, rows, offset), take)
            part = parts[k].at[p * take : (p + 1) * take]
            part[:, 0 : 2 * KW] = dot_nt(nT[at, :], gkv[...]).astype(BF16)
            part[:, 2 * KW :] = column[at, :]


def unpack_kernel(nd, pack_0, pack_1, gate, up, down_t):
    rows = gate.shape[0]
    quarter = down_t.shape[1] // 4
    width = nd * quarter
    half, rest, tail = quarter // 2, down_t.shape[0] - width, 2 * rows + quarter
    size = tail + half
    for core, packs in enumerate((pack_0, pack_1)):
        for f in range(2):
            pack = packs[f * size : (f + 1) * size].astype(F32)
            at = core * 2 * quarter + f * quarter
            for j in range(nd):
                dst = slice(j * 4 * quarter + at, j * 4 * quarter + at + quarter)
                src = slice(j * quarter, (j + 1) * quarter)
                gate[:, dst] = pack[0:rows, src]
                up[:, dst] = pack[rows : 2 * rows, src]
            last = jnp.concatenate([pack[tail:, 0:rest], pack[tail:, rest:]], axis=0)
            block = jnp.concatenate([pack[2 * rows : tail], last], axis=1)
            down_t[:, at : at + quarter] = block.T


def local(
    nd, nc, tokens, positions, w_qkv, w_out, w_gate, w_up, w_down, g_attn, g_mlp, grad_out
):
    plan = Plan(nd, nc)
    idx = plan.owners()
    x = tokens[0].T
    dy = grad_out[0].T
    model, count = x.shape
    shard = w_qkv.shape[0]
    offset, take = row_split(shard)
    start = plan.core * offset
    run = count // 2
    width = QW + 2 * KW

    def slice_rows(a):
        return lax.dynamic_slice_in_dim(a, start, take, 0)

    pad = jnp.zeros((take, 62), BF16)
    qkv_part = jnp.concatenate(
        [slice_rows(w_qkv), slice_rows(g_attn)[:, None], slice_rows(g_mlp)[:, None], pad], axis=1
    )
    dy_sib = plan.swap(dy)
    qkv_task = Task(plan.spread(qkv_part, plan.kd, plan.hop_d)).go(2)
    size = 2 * shard + w_down.shape[0] * 3 // 8
    mlp_width = w_gate.shape[1] // 4
    (pack,) = call(
        functools.partial(pack_kernel, nd),
        "pack",
        [((2 * size + shard * 3 // 2, mlp_width), BF16)],
        [idx, w_gate, w_up, w_down.T, w_out],
        smem=1,
        limit=12,
        us=4,
    )
    plan.gates = (pack,)
    qkv_parts = qkv_task.finish()
    plan.gates = ()
    qkv_sib = [plan.swap(p) for p in qkv_parts[:-1]]
    qkv_parts[-1] = after(qkv_parts[-1], dy_sib, *qkv_sib)
    qkv_sib.append(plan.swap(qkv_parts[-1]))
    plan.gates = qkv_parts[1:]
    pack_task = Task(plan.spread(pack, plan.kd, plan.hop_d)).go(2)

    pos = positions[0]
    q_blocks = pos[::run] // run
    half = HEAD_SIZE // 2
    freqs = THETA ** (-(jnp.arange(half).astype(F32) * 2.0) / HEAD_SIZE)
    angles = freqs[:, None] * pos.astype(F32)[None, :]
    cos, sin = jnp.cos(angles), jnp.sin(angles)

    normed, qT, kv, w_full, gains = call(
        functools.partial(project_kernel, nd),
        "project",
        [
            ((model, count), BF16),
            ((QW, count), BF16),
            ((2 * KW + 16, count), BF16),
            ((model, width + 64), BF16),
            ((model, 128), BF16),
        ],
        [after(idx, pack, dy_sib), pos[None], cos, sin, x] + qkv_parts + qkv_sib,
        smem=1,
        limit=20,
        us=6,
    )

    pieces = 1 << plan.kz
    plan.gates = (gains,)
    kv_sib = {0: plan.swap(kv)}
    kv_own = {0: kv}
    for j in range(plan.kz):
        kv_own[1 << j] = plan.hop_z(kv, j)
    qs = [qT, plan.swap(qT)]
    all_blocks = jnp.concatenate([q_blocks, kv_sib[0][2 * KW, ::run].astype(jnp.int32)])
    state = forward_wave(q_blocks, qT, [kv, kv_sib[0]], None, False, 8)
    for w in range(1, pieces):
        if w == 1:
            *state, kv_own[1], kv_own[2] = settle((*state, kv_own[1], kv_own[2]), pack_task)
        plan.gates = (state[0],)
        if w == 1:
            pack_task.go()
        for j in range(w.bit_length(), plan.kz):
            if w + (1 << j) not in kv_own:
                kv_own[w + (1 << j)] = plan.hop_z(kv_own[w], j)
        if w not in kv_sib:
            kv_sib[w] = plan.swap(kv_own[w])
        blocks = q_blocks
        if w == 1 and pieces > 2:
            kv_sib[2] = plan.swap(kv_own[2])
            blocks = after(blocks, kv_sib[2])
        state = forward_wave(blocks, qT, [kv_own[w], kv_sib[w]], state, w == pieces - 1, 8)
    pack_parts = pack_task.finish()
    oT, lse = settle(state, pack_task)

    plan.gates = (lse,)
    mid, normed_two, w_out_full = call(
        functools.partial(middle_kernel, nd),
        "middle",
        [((model, count), F32), ((model, count), BF16), ((QW, model), BF16)],
        [idx, x, oT, gains] + pack_parts,
        smem=1,
        limit=24,
        us=5,
    )
    normed_two_sib = plan.swap(normed_two)
    tall = nd * size
    got = call(
        functools.partial(mlp_kernel, nd),
        "mlp",
        [((model, count), BF16)] * 4 + [((tall, mlp_width), BF16)] * 2,
        [idx, normed_two, normed_two_sib, dy, dy_sib] + pack_parts,
        smem=1,
        scratch=[
            pltpu.VMEM((model, mlp_width), BF16),
            pltpu.VMEM((model, mlp_width), BF16),
            pltpu.VMEM((mlp_width, model), BF16),
            pltpu.VMEM((mlp_width, model), BF16),
            pltpu.VMEM((mlp_width, model), BF16),
            pltpu.VMEM((model, mlp_width), BF16),
            pltpu.VMEM((model, 2 * count), BF16),
            pltpu.VMEM((model, 2 * count), BF16),
            pltpu.VMEM((mlp_width, 2 * count), BF16),
            pltpu.VMEM((mlp_width, 2 * count), BF16),
            pltpu.VMEM((mlp_width, 2 * count), BF16),
        ],
        limit=44,
        us=36,
    )
    sums, (near, far) = got[:4], got[4:]
    plan.gates = ()
    gn_got = plan.swap(sums[3])
    pack_total = Task(plan.reduce_all(near, far)).go(1)
    turned = call(
        turn_kernel,
        "turn",
        [
            ((model, count), F32),
            ((model, count), BF16),
            ((QW, count), BF16),
            ((32, count), F32),
            ((model, 128), BF16),
        ],
        [idx, mid, gains, sums[2], gn_got, dy, oT, lse, w_out_full],
        smem=1,
        limit=30,
        us=8,
    )
    grad_mid, grad_half, doT, stats, column = turned
    plan.gates = (stats,)
    dos = [doT, plan.swap(doT)]
    both_stats = [stats, plan.swap(stats)]

    dq = None
    totals = {p: [] for p in range(pieces)}
    moved = []
    top = pieces - 1
    waits = {top - 1: (pack_total,), top - 2: (pack_total,)}
    for p in reversed(range(pieces)):
        got = backward_wave(
            all_blocks, qs, dos, both_stats, kv_own[p], totals[p] if p else [], dq, p == 0, 10
        )
        arrived = moved[-1:]
        got = settle(got, *waits.get(p, ()), *arrived)
        dkv = got[-1]
        plan.gates = (dkv,)
        if p:
            dq = got[0]
            j = p.bit_length() - 1
            moved.append(plan.hop_z(dkv, j))
            totals[p - (1 << j)].append(moved[-1])
        else:
            totals[0].append(dkv)
        if p in (top - 1, top - 2):
            pack_total.go(1)
    dq_got = plan.swap(got[1])
    wide = -(-(2 * model + 128) // 128) * 128
    stacked = ((nd * take, wide), BF16)
    gq, *parts = call(
        functools.partial(query_kernel, nd),
        "query",
        [((QW, count), BF16), stacked, stacked],
        [idx, got[0], dq_got, cos, sin, normed, oT, grad_half, column],
        smem=1,
        limit=22,
        us=4,
    )
    plan.gates = (gq,)

    def both_cores(own, stacked):
        other = plan.swap(stacked)
        half = own.shape[0] // 2
        return add(own[:half], other[:half]), add(own[half:], other[half:])

    gq, *parts = settle((gq, *parts), pack_total)
    near, far = both_cores(*parts)
    query_total = Task(plan.reduce_all(near, far, small=True)).go(1)
    pack_total.go(1)
    last_idx = after(idx, far)
    terms = totals[0]
    stacked = ((nd * take, 2 * KW + 128), BF16)
    grad_tokens, *parts = call(
        functools.partial(last_kernel, nd, len(terms)),
        "last",
        [((model, count), BF16), stacked, stacked],
        [last_idx, x, gains, cos, sin, normed, gq, w_full, grad_mid] + terms,
        smem=1,
        scratch=[pltpu.VMEM((width + 64, count), BF16), pltpu.VMEM((model, 128), BF16)],
        limit=28,
        us=6,
    )
    plan.gates = (parts[0],)
    out_got = plan.swap(sums[1])
    output = (mid + (sums[0].astype(F32) + out_got.astype(F32))).astype(BF16)
    kv_total = Task(plan.reduce_all(*both_cores(*parts), small=True))
    kv_halves = kv_total.finish()
    query_halves = query_total.finish()
    gate, up, down = call(
        functools.partial(unpack_kernel, nd),
        "unpack",
        [(w.shape, F32) for w in (w_gate, w_up, w_down.T)],
        list(pack_total.finish()),
        limit=24,
        us=6,
    )

    def whole(halves):
        low, high = halves
        return jnp.concatenate([low, high[2 * take - shard :]], axis=0).astype(F32)

    query_whole = whole(query_halves)
    kv_whole = whole(kv_halves)
    qkv_whole = jnp.concatenate(
        [query_whole[:, model + 128 : 2 * model + 128], kv_whole[:, : 2 * KW]], axis=1
    )
    return (
        output.T[None],
        grad_tokens.T[None],
        qkv_whole,
        query_whole[:, :model],
        gate,
        up,
        down.T,
        kv_whole[:, 2 * KW],
        query_whole[:, model],
    )


def solution(mesh):
    rows = P("dp", None)
    stored = P("dp", "ctx", None)
    vector = P("dp")
    return jax.shard_map(
        functools.partial(local, mesh.shape["dp"], mesh.shape["ctx"]),
        mesh=mesh,
        in_specs=(stored, P("dp", "ctx"), rows, rows, rows, rows, rows, vector, vector, stored),
        out_specs=(stored, stored, rows, rows, rows, rows, rows, vector, vector),
        check_vma=False,
    )
```

```python
import functools

import jax
import jax.numpy as jnp
from jax import lax
from jax.experimental import pallas as pl
from jax.experimental.pallas import tpu as pltpu
from jax.sharding import PartitionSpec as P

QUERY_HEADS = 15
KEY_VALUE_HEADS = 5
HEAD_SIZE = 64
GROUPS = QUERY_HEADS // KEY_VALUE_HEADS
QW = QUERY_HEADS * HEAD_SIZE
KW = KEY_VALUE_HEADS * HEAD_SIZE
EPS = 1e-05
THETA = 10000.0
MASK_FILL = -1e30
F32 = jnp.float32
BF16 = jnp.bfloat16
NT = (((1,), (1,)), ((), ()))
CORES = 2
SWAP_ROWS = 16
MIB = 2**20


def dot(a, b):
    return jnp.dot(a, b, preferred_element_type=F32)


def dot_nt(a, b):
    return lax.dot_general(a, b, NT, preferred_element_type=F32)


def call(kernel, name, outs, args, smem=0, scratch=(), limit=32, us=10, aliases=None):
    specs = [pl.BlockSpec(memory_space=pltpu.SMEM)] * smem
    specs += [pl.BlockSpec(memory_space=pltpu.VMEM)] * (len(args) - smem)
    return pl.pallas_call(
        kernel,
        out_shape=tuple(jax.ShapeDtypeStruct(s, d) for s, d in outs),
        in_specs=specs,
        out_specs=tuple(pl.BlockSpec(memory_space=pltpu.VMEM) for _ in outs),
        scratch_shapes=list(scratch),
        compiler_params=pltpu.CompilerParams(vmem_limit_bytes=limit * MIB),
        cost_estimate=pl.CostEstimate(
            flops=int(us * 1e7), bytes_accessed=0, transcendentals=0
        ),
        input_output_aliases=aliases or {},
        name=name,
    )(*args)


class Plan:
    def __init__(self, nd, nc):
        self.nd, self.nz = nd, nc // CORES
        self.kd, self.kz = nd.bit_length() - 1, self.nz.bit_length() - 1
        self.core = lax.axis_index("ctx") % CORES
        self.z = lax.axis_index("ctx") // CORES
        self.d = lax.axis_index("dp")
        self.gates = ()

    def order(self, k, core):
        return [(j + core) % k for j in range(k)]

    def masks(self, k, core):
        order = self.order(k, core)
        return [
            sum(1 << order[j] for j in range(k) if (p >> j) & 1) for p in range(1 << k)
        ]

    def place(self, d, z, c):
        return (d * self.nz + z) * CORES + c

    def everywhere(self):
        for d in range(self.nd):
            for z in range(self.nz):
                for c in range(CORES):
                    yield d, z, c

    def hop_d(self, x, j):
        perm = [
            (
                self.place(d, z, c),
                self.place(d ^ (1 << self.order(self.kd, c)[j]), z, c),
            )
            for d, z, c in self.everywhere()
        ]
        return lax.ppermute(after(x, *self.gates), ("dp", "ctx"), perm)

    def hop_z(self, x, j):
        perm = [
            (
                self.place(d, z, c),
                self.place(d, z ^ (1 << self.order(self.kz, c)[j]), c),
            )
            for d, z, c in self.everywhere()
        ]
        return lax.ppermute(after(x, *self.gates), ("dp", "ctx"), perm)

    def swap(self, x):
        perm = [(self.place(d, z, c), self.place(d, z, 1 - c)) for d, z, c in self.everywhere()]
        return lax.ppermute(after(x, *self.gates), ("dp", "ctx"), perm)

    def spread(self, x, k, hop):
        held = [x]
        for j in range(k):
            for h in list(held):
                held.append(hop(h, j))
                yield held[-1]
        return held

    def fold(self, near, far, k, hop):
        terms = [near]
        for j in reversed(range(k)):
            got = hop(far, j)
            yield got
            got = after(got, *self.gates)
            terms.append(got)
            if j:
                half = got.shape[0] // 2
                far = add(*[t[half:] for t in terms])
                terms = [t[:half] for t in terms]
        return add(*terms)

    def double_z(self, x):
        for j in range(self.kz):
            got = self.hop_z(x, j)
            yield got
            x = add(x, after(got, *self.gates))
        return x

    def owners(self):
        m0 = jnp.array(self.masks(self.kd, 0), jnp.int32)
        m1 = jnp.array(self.masks(self.kd, 1), jnp.int32)
        mine = jnp.where(self.core == 0, m0, m1) ^ self.d
        other = jnp.where(self.core == 0, m1, m0) ^ self.d
        return jnp.concatenate([self.core[None], mine, other]).astype(jnp.int32)

    def total_z(self, x):
        sizes = []
        for j in reversed(range(self.kz)):
            order = jnp.where(
                self.core == 0, self.order(self.kz, 0)[j], self.order(self.kz, 1)[j]
            )
            bit = (self.z >> order) & 1
            rows = x.shape[0]
            size = -(-rows // 16) * 8
            keep = lax.dynamic_slice_in_dim(x, bit * (rows - size), size, 0)
            send = lax.dynamic_slice_in_dim(x, (1 - bit) * (rows - size), size, 0)
            sizes.append((bit, rows, size))
            got = self.hop_z(send, j)
            yield got
            got = after(got, *self.gates)
            x = add(keep, got)
        for j in range(self.kz):
            bit, rows, size = sizes.pop()
            got = self.hop_z(x, j)
            yield got
            low = jnp.where(bit == 0, x, got)
            high = jnp.where(bit == 0, got, x)
            x = jnp.concatenate([low[: rows - size], high], axis=0)
        return x

    def reduce_all(self, near, far, small=False):
        x = yield from self.fold(near, far, self.kd, self.hop_d)
        x = yield from (self.double_z if small else self.total_z)(x)
        other = self.swap(x)
        yield other
        return jnp.where(self.core == 0, x, other), jnp.where(self.core == 0, other, x)


class Task:
    def __init__(self, steps):
        self.steps, self.out, self.done, self.result = steps, [], False, None

    def go(self, n=1000):
        while n > 0 and not self.done:
            try:
                self.out.append(next(self.steps))
            except StopIteration as stop:
                self.done, self.result = True, stop.value
            n -= 1
        return self

    def finish(self):
        return self.go().result


def settle(outs, *tasks):
    waited = []
    for task in tasks:
        if isinstance(task, Task):
            waited += task.out
            task.out = []
        else:
            waited.append(task)
    if not waited:
        return tuple(outs)
    return lax.optimization_barrier((*outs, *waited))[: len(outs)]


def after(x, *tasks):
    return settle((x,), *tasks)[0]


def add(*terms):
    if len(terms) == 1:
        return terms[0]
    return functools.reduce(lambda a, b: a + b, [t.astype(F32) for t in terms]).astype(BF16)


def row_split(rows):
    offset = rows // 2 // 16 * 16
    return offset, rows - offset


def start_row(idx, slot, parity, rows, offset):
    return pl.multiple_of(idx[slot] * rows + parity * offset, 8)


def pack_kernel(nd, idx, gate, up, down_t, w_out, pack):
    rows, width = gate.shape[0], pack.shape[1]
    down = down_t[...].T
    shard, model = down.shape
    quarter = shard // 4
    rest, half = model - width, quarter // 2
    for core in range(CORES):

        @pl.when(idx[0] == core)
        def _(core=core):
            for f in range(2):
                at = core * 2 * quarter + f * quarter
                out = pack.at[pl.ds(f * (2 * rows + quarter + half), 2 * rows + quarter + half)]
                for j in range(nd):
                    src = slice(j * shard + at, j * shard + at + quarter)
                    dst = slice(j * quarter, (j + 1) * quarter)
                    out[0:rows, dst] = gate[:, src]
                    out[rows : 2 * rows, dst] = up[:, src]
                block = down[at : at + quarter, :]
                tail = 2 * rows + quarter
                out[2 * rows : tail, :] = block[:, :width]
                out[tail : tail + half, 0:rest] = block[:half, width:]
                out[tail : tail + half, rest:] = block[half:, width:]

    end = pack.shape[0] - rows - rows // 2
    half = rows // 2
    pack[end : end + rows, :] = w_out[:, :width]
    pack[end + rows :, 0:rest] = w_out[0:half, width:]
    pack[end + rows :, rest:] = w_out[half:, width:]


def gain_column(gain_ref, which):
    lane = (QW + 2 * KW) % 128 + which
    return gain_ref[...].astype(F32)[:, lane : lane + 1]


def project_kernel(nd, idx, pos, cos, sin, x_ref, *refs):
    pieces = refs[: 2 * nd]
    normed_ref, q_ref, kv_ref, w_ref, gain_ref = refs[2 * nd :]
    model = x_ref.shape[0]
    rows = model // nd
    offset, take = row_split(rows)
    core = idx[0]
    for p in range(nd):
        w_ref[pl.ds(start_row(idx, 1 + p, core, rows, offset), take), :] = pieces[p][...]
        w_ref[pl.ds(start_row(idx, 1 + nd + p, 1 - core, rows, offset), take), :] = pieces[
            nd + p
        ][...]
    low = (QW + 2 * KW) // 128 * 128
    gain_ref[...] = w_ref[:, low : low + 128]
    x = x_ref[...].astype(F32)
    factor = lax.rsqrt(jnp.mean(x * x, axis=0, keepdims=True) + EPS)
    normed = (x * factor * gain_column(gain_ref, 0)).astype(BF16)
    normed_ref[...] = normed
    normed = normed.T
    half = HEAD_SIZE // 2
    c, s = cos[...], sin[...]
    heads = 10
    for b in range(0, w_ref.shape[1], heads * HEAD_SIZE):
        block = dot(normed, w_ref[:, b : b + heads * HEAD_SIZE]).T
        for i in range(heads):
            head = b // HEAD_SIZE + i
            if head >= QUERY_HEADS + 2 * KEY_VALUE_HEADS:
                break
            u1 = block[i * HEAD_SIZE : i * HEAD_SIZE + half]
            u2 = block[i * HEAD_SIZE + half : (i + 1) * HEAD_SIZE]
            if head < QUERY_HEADS + KEY_VALUE_HEADS:
                u1, u2 = u1 * c - u2 * s, u2 * c + u1 * s
            both = jnp.concatenate([u1, u2], axis=0).astype(BF16)
            if head < QUERY_HEADS:
                q_ref[head * HEAD_SIZE : (head + 1) * HEAD_SIZE] = (
                    both.astype(F32) * HEAD_SIZE**-0.5
                ).astype(BF16)
            else:
                at = (head - QUERY_HEADS) * HEAD_SIZE
                kv_ref[at : at + HEAD_SIZE] = both
    run = x_ref.shape[1] // 2
    blocks = jnp.broadcast_to(
        (pos[...] // run).astype(F32), (kv_ref.shape[0] - 2 * KW, x_ref.shape[1])
    )
    kv_ref[2 * KW :, :] = blocks.astype(BF16)


def list_pairs(q_blocks, kv_s, count, run, todo):
    n = jnp.int32(0)
    for rank in range(count):
        for part in range(2):
            tile = kv_s[rank, 2 * KW : 2 * KW + 16, part * run : part * run + 128]
            block = jnp.max(tile.astype(F32)).astype(jnp.int32)
            for r in range(2):
                active = block < q_blocks[r]

                @pl.when(active)
                def _(n=n, code=r * 256 + rank * 2 + part):
                    todo[n] = code

                n = n + active.astype(jnp.int32)
    return n


def each_pair(todo, n, run, pair):
    def body(i, _):
        code = todo[i]
        r = code // 256
        block = code % 256
        pair(
            block // 2,
            pl.multiple_of((block % 2) * run, run),
            pl.multiple_of(r * run, run),
            False,
        )
        return 0

    lax.fori_loop(0, n, body, 0)


def forward_kernel(count, first, last, run, q_blocks, qT, *refs):
    kvs, refs = refs[:count], refs[count:]
    if not first:
        m_in, l_in, acc_in = refs[:3]
        refs = refs[3:]
    if last:
        o_ref, lse_ref, kv_s, m_s, l_s, acc_s, todo = refs
    else:
        m_s, l_s, acc_s, kv_s, todo = refs
    for i in range(count):
        kv_s[i] = kvs[i][...]
    if not first:
        m_s[...] = m_in[...]
        l_s[...] = l_in[...]
        acc_s[...] = acc_in[...]
    n = list_pairs(q_blocks, kv_s, count, run, todo)
    keep = lax.broadcasted_iota(jnp.int32, (run, run), 0) <= lax.broadcasted_iota(
        jnp.int32, (run, run), 1
    )

    def pair(rank, ko, qo, diag):
        def scores(hd):
            h = hd // GROUPS
            k = kv_s[rank, h * HEAD_SIZE : (h + 1) * HEAD_SIZE, pl.ds(ko, run)].T
            return dot(k, qT[hd * HEAD_SIZE : (hd + 1) * HEAD_SIZE, pl.ds(qo, run)])

        def flush(hd, p, shrink):
            h = KEY_VALUE_HEADS + hd // GROUPS
            vT = kv_s[rank, h * HEAD_SIZE : (h + 1) * HEAD_SIZE, pl.ds(ko, run)]
            o = dot(vT, p)
            rows = slice(hd * HEAD_SIZE, (hd + 1) * HEAD_SIZE)
            if shrink is not None:
                o = acc_s[rows, pl.ds(qo, run)] * shrink + o
            acc_s[rows, pl.ds(qo, run)] = o

        if not diag:
            m_all = m_s[:, pl.ds(qo, run)]
            l_all = l_s[:, pl.ds(qo, run)]

        def top(hd, s):
            if diag:
                s = jnp.where(keep, s, MASK_FILL)
            m = jnp.max(s, axis=0, keepdims=True)
            if not diag:
                m = jnp.maximum(m_all[hd : hd + 1], m)
            return s, m

        ms, ls, pending = [], [], None
        current = top(0, scores(0))
        following = scores(1)
        for hd in range(QUERY_HEADS):
            s, m = current
            if hd + 1 < QUERY_HEADS:
                current = top(hd + 1, following)
            if hd + 2 < QUERY_HEADS:
                following = scores(hd + 2)
            if pending is not None:
                flush(*pending)
            p = jnp.exp(s - m)
            total = jnp.sum(p, axis=0, keepdims=True)
            shrink = None
            if not diag:
                shrink = jnp.exp(m_all[hd : hd + 1] - m)
                total = l_all[hd : hd + 1] * shrink + total
            ms.append(m)
            ls.append(total)
            pending = (hd, p.astype(BF16), shrink)
        flush(*pending)
        m_s[:, pl.ds(qo, run)] = jnp.concatenate(ms + ms[-1:], 0)
        l_s[:, pl.ds(qo, run)] = jnp.concatenate(ls + ls[-1:], 0)

    if first:
        for r in range(2):
            pair(0, r * run, r * run, True)
    each_pair(todo, n, run, pair)
    if last:
        lse_ref[...] = m_s[...] + jnp.log(l_s[...])
        for hd in range(QUERY_HEADS):
            rows = slice(hd * HEAD_SIZE, (hd + 1) * HEAD_SIZE)
            o_ref[rows, :] = (acc_s[rows, :] / l_s[hd : hd + 1, :]).astype(BF16)


def forward_wave(q_blocks, qT, kvs, state, last, us):
    tokens = qT.shape[1]
    stats = pltpu.VMEM((16, tokens), F32)
    kv_s = pltpu.VMEM((len(kvs),) + kvs[0].shape, BF16)
    todo = pltpu.SMEM((4 * len(kvs),), jnp.int32)
    first = state is None
    args = [q_blocks, qT] + list(kvs) + ([] if first else list(state))
    if last:
        outs = [((QW, tokens), BF16), ((16, tokens), F32)]
        scratch = [kv_s, stats, stats, pltpu.VMEM((QW, tokens), F32), todo]
    else:
        outs = [((16, tokens), F32), ((16, tokens), F32), ((QW, tokens), F32)]
        scratch = [kv_s, todo]
    return call(
        functools.partial(forward_kernel, len(kvs), first, last, tokens // 2),
        "attention_forward",
        outs,
        args,
        smem=1,
        scratch=scratch,
        limit=12 + 2 * len(kvs),
        us=us,
    )


def backward_kernel(first, last, terms, run, q_blocks, *refs):
    q_own, q_sib, do_own, do_sib, st_own, st_sib, kv = refs[:7]
    before, refs = refs[7 : 7 + terms], refs[7 + terms :]
    if not first:
        dq_in, refs = refs[0], refs[1:]
    if last:
        dq_own, dq_sib, out, dq_s, q_s, do_s, st_s, dkv_s, todo = refs
    else:
        dq_s, out, q_s, do_s, st_s, dkv_s, todo = refs
    for s, (q, do, st) in enumerate(((q_own, do_own, st_own), (q_sib, do_sib, st_sib))):
        q_s[s] = q[...]
        do_s[s] = do[...]
        st_s[s] = st[...]
    if terms:
        dkv_s[...] = functools.reduce(lambda a, b: a + b, [t[...].astype(F32) for t in before])
    else:
        dkv_s[...] = jnp.zeros_like(dkv_s)
    dq_s[...] = jnp.zeros_like(dq_s) if first else dq_in[...]
    n = jnp.int32(0)
    for part in range(2):
        tile = kv[2 * KW : 2 * KW + 16, part * run : part * run + 128]
        block = jnp.max(tile.astype(F32)).astype(jnp.int32)
        for r in range(4):
            active = block < q_blocks[r]

            @pl.when(active)
            def _(n=n, code=r * 2 + part):
                todo[n] = code

            n = n + active.astype(jnp.int32)
    keep = lax.broadcasted_iota(jnp.int32, (run, run), 0) <= lax.broadcasted_iota(
        jnp.int32, (run, run), 1
    )

    def pair(who, ko, qo, diag):
        lse_all = st_s[who, 0:16, pl.ds(qo, run)]
        delta_all = st_s[who, 16:32, pl.ds(qo, run)]

        def rows(h):
            return slice(h * HEAD_SIZE, (h + 1) * HEAD_SIZE)

        def opening(hd):
            h = hd // GROUPS
            k = kv[rows(h), pl.ds(ko, run)].T
            v = kv[rows(KEY_VALUE_HEADS + h), pl.ds(ko, run)].T
            return (
                dot(k, q_s[who, rows(hd), pl.ds(qo, run)]),
                dot(v, do_s[who, rows(hd), pl.ds(qo, run)]),
            )

        def closing(hd, p, ds):
            h = hd // GROUPS
            q = q_s[who, rows(hd), pl.ds(qo, run)]
            do = do_s[who, rows(hd), pl.ds(qo, run)]
            kT = kv[rows(h), pl.ds(ko, run)]
            dkv_s[rows(KEY_VALUE_HEADS + h), pl.ds(ko, run)] += dot_nt(do, p)
            dkv_s[rows(h), pl.ds(ko, run)] += dot_nt(q, ds)
            dq_s[who, rows(hd), pl.ds(qo, run)] += dot(kT, ds)

        following, pending = opening(0), None
        for hd in range(QUERY_HEADS):
            s, dp = following
            if hd + 1 < QUERY_HEADS:
                following = opening(hd + 1)
            if pending is not None:
                closing(*pending)
            p = jnp.exp(s - lse_all[hd : hd + 1])
            if diag:
                p = jnp.where(keep, p, 0.0)
            ds = (p * (dp - delta_all[hd : hd + 1])).astype(BF16)
            pending = (hd, p.astype(BF16), ds)
        closing(*pending)

    if last:
        for r in range(2):
            pair(0, r * run, r * run, True)

    def body(i, _):
        code = todo[i]
        r = code // 2
        pair(
            r // 2,
            pl.multiple_of((code % 2) * run, run),
            pl.multiple_of((r % 2) * run, run),
            False,
        )
        return 0

    lax.fori_loop(0, n, body, 0)
    out[...] = dkv_s[...].astype(BF16)
    if last:
        dq_own[...] = dq_s[0]
        dq_sib[...] = dq_s[1].astype(BF16)


def backward_wave(q_blocks, qs, dos, stats, kv, before, dq, last, us):
    tokens = kv.shape[1]
    both = (2, QW, tokens)
    args = [q_blocks, *qs, *dos, *stats, kv, *before] + ([] if dq is None else [dq])
    scratch = [
        pltpu.VMEM(both, BF16),
        pltpu.VMEM(both, BF16),
        pltpu.VMEM((2, 32, tokens), F32),
        pltpu.VMEM((2 * KW, tokens), F32),
        pltpu.SMEM((16,), jnp.int32),
    ]
    out = ((2 * KW, tokens), BF16)
    if last:
        outs = [((QW, tokens), F32), ((QW, tokens), BF16), out]
        scratch = [pltpu.VMEM(both, F32)] + scratch
    else:
        outs = [(both, F32), out]
    return call(
        functools.partial(backward_kernel, dq is None, last, len(before), tokens // 2),
        "attention_backward",
        outs,
        args,
        smem=1,
        scratch=scratch,
        limit=28,
        us=us,
    )


def middle_kernel(nd, idx, x_ref, oT, gain_ref, *refs):
    pieces = refs[:nd]
    mid_ref, normed_ref, w_ref = refs[nd:]
    rows, width = w_ref.shape[0] // nd, pieces[0].shape[1]
    rest, half = w_ref.shape[1] - width, rows // 2
    end = pieces[0].shape[0] - rows - half
    for p in range(nd):
        at = pl.multiple_of(idx[1 + p] * rows, 8)
        w_ref[pl.ds(at, rows), 0:width] = pieces[p][end : end + rows]
        w_ref[pl.ds(at, half), width:] = pieces[p][end + rows :, 0:rest]
        w_ref[pl.ds(pl.multiple_of(at + half, 8), half), width:] = pieces[p][end + rows :, rest:]
    mid = x_ref[...].astype(F32) + dot(w_ref[...].T, oT[...])
    mid_ref[...] = mid
    factor = lax.rsqrt(jnp.mean(mid * mid, axis=0, keepdims=True) + EPS)
    normed_ref[...] = (mid * factor * gain_column(gain_ref, 1)).astype(BF16)


def mlp_kernel(nd, idx, n_own, n_sib, dy_own, dy_sib, *refs):
    pieces, sums, stacks = refs[:nd], refs[nd : nd + 4], refs[nd + 4 : nd + 6]
    wg, wu, wd, wgT, wuT, wdT, nT, dyT, actT, dg_s, du_s = refs[nd + 6 :]
    model = wg.shape[0]
    rows, quarter, width = model // nd, wd.shape[0] // nd, wd.shape[0]
    half, rest, tail = quarter // 2, model - width, 2 * rows + quarter
    size = tail + half
    tokens = n_own.shape[1]
    nT[:, 0:tokens] = n_own[...]
    nT[:, tokens:] = n_sib[...]
    dyT[:, 0:tokens] = dy_own[...]
    dyT[:, tokens:] = dy_sib[...]
    step = 256
    for f in range(2):
        for p in range(nd):
            d = idx[1 + p]
            piece = pieces[p].at[pl.ds(f * size, size)]
            at = pl.multiple_of(d * rows, 8)
            wg[pl.ds(at, rows), :] = piece[0:rows]
            wu[pl.ds(at, rows), :] = piece[rows : 2 * rows]
            at = pl.multiple_of(d * quarter, 16)
            wd[pl.ds(at, quarter), 0:width] = piece[2 * rows : tail]
            wd[pl.ds(at, half), width:] = piece[tail:size, 0:rest]
            at = pl.multiple_of(d * quarter + half, 8)
            wd[pl.ds(at, half), width:] = piece[tail:size, rest:]
        wgT[...] = wg[...].T
        wuT[...] = wu[...].T
        wdT[...] = wd[...].T

        def opening(at):
            n, dy = nT[:, at : at + step], dyT[:, at : at + step]
            return dot(wgT[...], n), dot(wuT[...], n), dot(wd[...], dy)

        following = opening(0)
        for at in range(0, 2 * tokens, step):
            g, u, ga = following
            if at + step < 2 * tokens:
                following = opening(at + step)
            s = jax.nn.sigmoid(g)
            gs = g * s
            act = (gs * u).astype(BF16)
            du = (ga * gs).astype(BF16)
            dg = (ga * u * (s + gs * (1.0 - s))).astype(BF16)
            actT[:, at : at + step] = act
            dg_s[:, at : at + step] = dg
            du_s[:, at : at + step] = du
            out = dot(wdT[...], act)
            gn = dot(wg[...], dg) + dot(wu[...], du)
            r, to = at // tokens, at % tokens
            if f:
                out = out + sums[r][:, to : to + step].astype(F32)
                gn = gn + sums[2 + r][:, to : to + step].astype(F32)
            sums[r][:, to : to + step] = out.astype(BF16)
            sums[2 + r][:, to : to + step] = gn.astype(BF16)
        wg[...] = dot_nt(nT[...], dg_s[...]).astype(BF16)
        wu[...] = dot_nt(nT[...], du_s[...]).astype(BF16)
        wd[...] = dot_nt(actT[...], dyT[...]).astype(BF16)
        for p in range(nd):
            d = idx[1 + p]
            grads = stacks[p // (nd // 2)].at[pl.ds((p % (nd // 2) * 2 + f) * size, size)]
            at = pl.multiple_of(d * rows, 8)
            grads[0:rows] = wg[pl.ds(at, rows), :]
            grads[rows : 2 * rows] = wu[pl.ds(at, rows), :]
            at = pl.multiple_of(d * quarter, 16)
            grads[2 * rows : tail] = wd[pl.ds(at, quarter), 0:width]
            grads[tail:, 0:rest] = wd[pl.ds(at, half), width:]
            at = pl.multiple_of(d * quarter + half, 8)
            grads[tail:, rest:] = wd[pl.ds(at, half), width:]


def norm_backward(x, gain, grad):
    factor = lax.rsqrt(jnp.mean(x * x, axis=0, keepdims=True) + EPS)
    scaled = grad * gain
    along = jnp.mean(scaled * x, axis=0, keepdims=True)
    grad_x = factor * scaled - x * (factor * factor * factor * along)
    grad_gain = jnp.sum(grad * x * factor, axis=1, keepdims=True)
    return grad_x, grad_gain


def turn_kernel(
    idx, mid_ref, gain_ref, gn_own, gn_got, dy_ref, oT, lse, w_ref, *refs
):
    gmid_ref, half_ref, doT, stats, column = refs
    stats[0:16, :] = lse[...]
    delta = stats.at[16:32]
    mid = mid_ref[...]
    grad = gn_own[...].astype(F32) + gn_got[...].astype(F32)
    grad_mid, grad_gain = norm_backward(mid, gain_column(gain_ref, 1), grad)
    grad_mid = grad_mid + dy_ref[...].astype(F32)
    gmid_ref[...] = grad_mid
    half = grad_mid.astype(BF16)
    half_ref[...] = half
    heads = dot(w_ref[...], half).astype(BF16)
    doT[...] = heads
    for hd in range(QUERY_HEADS):
        rows = slice(hd * HEAD_SIZE, (hd + 1) * HEAD_SIZE)
        delta[hd : hd + 1, :] = jnp.sum(
            oT[rows, :].astype(F32) * heads[rows].astype(F32), axis=0, keepdims=True
        )
    delta[QUERY_HEADS:, :] = jnp.zeros_like(delta[QUERY_HEADS:, :])
    column[...] = jnp.broadcast_to(grad_gain, column.shape).astype(BF16)


def unrotate(head, cos, sin):
    half = HEAD_SIZE // 2
    g1, g2 = head[:half], head[half:]
    return jnp.concatenate([g1 * cos + g2 * sin, g2 * cos - g1 * sin], axis=0)


def query_kernel(nd, idx, dq, dq_got, cos, sin, nT, oT, half_ref, column, gq_ref, *parts):
    c, s = cos[...], sin[...]
    for hd in range(QUERY_HEADS):
        rows = slice(hd * HEAD_SIZE, (hd + 1) * HEAD_SIZE)
        gq_ref[rows, :] = unrotate(
            (dq[rows, :] + dq_got[rows, :].astype(F32)) * HEAD_SIZE**-0.5, c, s
        ).astype(BF16)
    model = half_ref.shape[0]
    rows = nT.shape[0] // nd
    offset, take = row_split(rows)
    for k in range(2):
        parity = idx[0] if k == 0 else 1 - idx[0]
        for p in range(nd):
            at = pl.ds(start_row(idx, 1 + k * nd + p, parity, rows, offset), take)
            part = parts[k].at[p * take : (p + 1) * take]
            part[:, 0:model] = dot_nt(oT[at, :], half_ref[...]).astype(BF16)
            part[:, model : model + 128] = column[at, :]
            part[:, model + 128 : 2 * model + 128] = dot_nt(nT[at, :], gq_ref[...]).astype(BF16)


def last_kernel(nd, terms, idx, x_ref, gain_ref, cos, sin, nT, gq, w_ref, gmid_ref, *refs):
    dkvs, refs = refs[:terms], refs[terms:]
    gx_ref, parts, gp, column = refs[0], refs[1:3], refs[3], refs[4]
    gkv = gp.at[QW : QW + 2 * KW]
    gp[0:QW] = gq[...]
    gp[QW + 2 * KW :] = jnp.zeros((gp.shape[0] - QW - 2 * KW, gp.shape[1]), BF16)
    c, s = cos[...], sin[...]
    for h in range(2 * KEY_VALUE_HEADS):
        rows = slice(h * HEAD_SIZE, (h + 1) * HEAD_SIZE)
        block = functools.reduce(lambda a, b: a + b, [t[rows, :].astype(F32) for t in dkvs])
        if h < KEY_VALUE_HEADS:
            block = unrotate(block, c, s)
        gkv[rows, :] = block.astype(BF16)
    wide = dot(w_ref[...], gp[...])
    x = x_ref[...].astype(F32)
    grad_x, grad_gain = norm_backward(x, gain_column(gain_ref, 0), wide)
    gx_ref[...] = (grad_x + gmid_ref[...]).astype(BF16)
    column[...] = jnp.broadcast_to(grad_gain, column.shape).astype(BF16)
    rows = nT.shape[0] // nd
    offset, take = row_split(rows)
    for k in range(2):
        parity = idx[0] if k == 0 else 1 - idx[0]
        for p in range(nd):
            at = pl.ds(start_row(idx, 1 + k * nd + p, parity, rows, offset), take)
            part = parts[k].at[p * take : (p + 1) * take]
            part[:, 0 : 2 * KW] = dot_nt(nT[at, :], gkv[...]).astype(BF16)
            part[:, 2 * KW :] = column[at, :]


def unpack_kernel(nd, pack_0, pack_1, gate, up, down_t):
    rows = gate.shape[0]
    quarter = down_t.shape[1] // 4
    width = nd * quarter
    half, rest, tail = quarter // 2, down_t.shape[0] - width, 2 * rows + quarter
    size = tail + half
    for core, packs in enumerate((pack_0, pack_1)):
        for f in range(2):
            pack = packs[f * size : (f + 1) * size].astype(F32)
            at = core * 2 * quarter + f * quarter
            for j in range(nd):
                dst = slice(j * 4 * quarter + at, j * 4 * quarter + at + quarter)
                src = slice(j * quarter, (j + 1) * quarter)
                gate[:, dst] = pack[0:rows, src]
                up[:, dst] = pack[rows : 2 * rows, src]
            last = jnp.concatenate([pack[tail:, 0:rest], pack[tail:, rest:]], axis=0)
            block = jnp.concatenate([pack[2 * rows : tail], last], axis=1)
            down_t[:, at : at + quarter] = block.T


def final_kernel(q_low, q_high, k_low, k_high, qkv, out, mlp_gain, attn_gain):
    skip = 2 * q_low.shape[0] - qkv.shape[0]
    model = out.shape[1]
    low = model // 128 * 128
    q = jnp.concatenate([q_low[...].astype(F32), q_high[...].astype(F32)[skip:]], axis=0)
    k = jnp.concatenate([k_low[...].astype(F32), k_high[...].astype(F32)[skip:]], axis=0)
    out[...] = q[:, :model]
    qkv[:, 0:QW] = q[:, model + 128 : model + 128 + QW]
    qkv[:, QW:] = k[:, 0 : 2 * KW]
    mlp_gain[...] = q[:, low : low + 128].T[model - low : model - low + 1]
    attn_gain[...] = k[:, 2 * KW :].T[0:1]


def local(
    nd, nc, tokens, positions, w_qkv, w_out, w_gate, w_up, w_down, g_attn, g_mlp, grad_out
):
    plan = Plan(nd, nc)
    idx = plan.owners()
    x = tokens[0].T
    dy = grad_out[0].T
    model, count = x.shape
    shard = w_qkv.shape[0]
    offset, take = row_split(shard)
    start = plan.core * offset
    run = count // 2
    width = QW + 2 * KW

    def slice_rows(a):
        return lax.dynamic_slice_in_dim(a, start, take, 0)

    pad = jnp.zeros((take, 62), BF16)
    qkv_part = jnp.concatenate(
        [slice_rows(w_qkv), slice_rows(g_attn)[:, None], slice_rows(g_mlp)[:, None], pad], axis=1
    )
    dy_sib = plan.swap(dy)
    qkv_task = Task(plan.spread(qkv_part, plan.kd, plan.hop_d)).go(2)
    size = 2 * shard + w_down.shape[0] * 3 // 8
    mlp_width = w_gate.shape[1] // 4
    (pack,) = call(
        functools.partial(pack_kernel, nd),
        "pack",
        [((2 * size + shard * 3 // 2, mlp_width), BF16)],
        [idx, w_gate, w_up, w_down.T, w_out],
        smem=1,
        limit=12,
        us=4,
    )
    plan.gates = (pack,)
    qkv_parts = qkv_task.finish()
    plan.gates = ()
    qkv_sib = [plan.swap(p) for p in qkv_parts[:-1]]
    qkv_parts[-1] = after(qkv_parts[-1], dy_sib, *qkv_sib)
    qkv_sib.append(plan.swap(qkv_parts[-1]))
    plan.gates = qkv_parts[1:]
    pack_task = Task(plan.spread(pack, plan.kd, plan.hop_d)).go(2)

    pos = positions[0]
    q_blocks = pos[::run] // run
    half = HEAD_SIZE // 2
    freqs = THETA ** (-(jnp.arange(half).astype(F32) * 2.0) / HEAD_SIZE)
    angles = freqs[:, None] * pos.astype(F32)[None, :]
    cos, sin = jnp.cos(angles), jnp.sin(angles)

    normed, qT, kv, w_full, gains = call(
        functools.partial(project_kernel, nd),
        "project",
        [
            ((model, count), BF16),
            ((QW, count), BF16),
            ((2 * KW + 16, count), BF16),
            ((model, width + 64), BF16),
            ((model, 128), BF16),
        ],
        [after(idx, pack, dy_sib), pos[None], cos, sin, x] + qkv_parts + qkv_sib,
        smem=1,
        limit=20,
        us=6,
    )

    pieces = 1 << plan.kz
    plan.gates = (gains,)
    kv_sib = {0: plan.swap(kv)}
    kv_own = {0: kv}
    for j in range(plan.kz):
        kv_own[1 << j] = plan.hop_z(kv, j)
    qs = [qT, plan.swap(qT)]
    all_blocks = jnp.concatenate([q_blocks, kv_sib[0][2 * KW, ::run].astype(jnp.int32)])
    state = forward_wave(q_blocks, qT, [kv, kv_sib[0]], None, False, 8)
    for w in range(1, pieces):
        if w == 1:
            *state, kv_own[1], kv_own[2] = settle((*state, kv_own[1], kv_own[2]), pack_task)
        plan.gates = (state[0],)
        if w == 1:
            pack_task.go()
        for j in range(w.bit_length(), plan.kz):
            if w + (1 << j) not in kv_own:
                kv_own[w + (1 << j)] = plan.hop_z(kv_own[w], j)
        if w not in kv_sib:
            kv_sib[w] = plan.swap(kv_own[w])
        blocks = q_blocks
        if w == 1 and pieces > 2:
            kv_sib[2] = plan.swap(kv_own[2])
            blocks = after(blocks, kv_sib[2])
        state = forward_wave(blocks, qT, [kv_own[w], kv_sib[w]], state, w == pieces - 1, 8)
    pack_parts = pack_task.finish()
    oT, lse = settle(state, pack_task)

    plan.gates = (lse,)
    mid, normed_two, w_out_full = call(
        functools.partial(middle_kernel, nd),
        "middle",
        [((model, count), F32), ((model, count), BF16), ((QW, model), BF16)],
        [idx, x, oT, gains] + pack_parts,
        smem=1,
        limit=24,
        us=5,
    )
    normed_two_sib = plan.swap(normed_two)
    tall = nd * size
    got = call(
        functools.partial(mlp_kernel, nd),
        "mlp",
        [((model, count), BF16)] * 4 + [((tall, mlp_width), BF16)] * 2,
        [idx, normed_two, normed_two_sib, dy, dy_sib] + pack_parts,
        smem=1,
        scratch=[
            pltpu.VMEM((model, mlp_width), BF16),
            pltpu.VMEM((model, mlp_width), BF16),
            pltpu.VMEM((mlp_width, model), BF16),
            pltpu.VMEM((mlp_width, model), BF16),
            pltpu.VMEM((mlp_width, model), BF16),
            pltpu.VMEM((model, mlp_width), BF16),
            pltpu.VMEM((model, 2 * count), BF16),
            pltpu.VMEM((model, 2 * count), BF16),
            pltpu.VMEM((mlp_width, 2 * count), BF16),
            pltpu.VMEM((mlp_width, 2 * count), BF16),
            pltpu.VMEM((mlp_width, 2 * count), BF16),
        ],
        limit=44,
        us=36,
    )
    sums, (near, far) = got[:4], got[4:]
    plan.gates = ()
    gn_got = plan.swap(sums[3])
    pack_total = Task(plan.reduce_all(near, far)).go(1)
    turned = call(
        turn_kernel,
        "turn",
        [
            ((model, count), F32),
            ((model, count), BF16),
            ((QW, count), BF16),
            ((32, count), F32),
            ((model, 128), BF16),
        ],
        [idx, mid, gains, sums[2], gn_got, dy, oT, lse, w_out_full],
        smem=1,
        limit=30,
        us=8,
    )
    grad_mid, grad_half, doT, stats, column = turned
    plan.gates = (stats,)
    dos = [doT, plan.swap(doT)]
    both_stats = [stats, plan.swap(stats)]

    dq = None
    totals = {p: [] for p in range(pieces)}
    moved = []
    top = pieces - 1
    waits = {top - 1: (pack_total,), top - 2: (pack_total,)}
    for p in reversed(range(pieces)):
        got = backward_wave(
            all_blocks, qs, dos, both_stats, kv_own[p], totals[p] if p else [], dq, p == 0, 10
        )
        arrived = moved[-1:]
        got = settle(got, *waits.get(p, ()), *arrived)
        dkv = got[-1]
        plan.gates = (dkv,)
        if p:
            dq = got[0]
            j = p.bit_length() - 1
            moved.append(plan.hop_z(dkv, j))
            totals[p - (1 << j)].append(moved[-1])
        else:
            totals[0].append(dkv)
        if p in (top - 1, top - 2):
            pack_total.go(1)
    dq_got = plan.swap(got[1])
    wide = -(-(2 * model + 128) // 128) * 128
    stacked = ((nd * take, wide), BF16)
    gq, *parts = call(
        functools.partial(query_kernel, nd),
        "query",
        [((QW, count), BF16), stacked, stacked],
        [idx, got[0], dq_got, cos, sin, normed, oT, grad_half, column],
        smem=1,
        limit=22,
        us=4,
    )
    plan.gates = (gq,)

    def both_cores(own, stacked):
        other = plan.swap(stacked)
        half = own.shape[0] // 2
        return add(own[:half], other[:half]), add(own[half:], other[half:])

    gq, *parts = settle((gq, *parts), pack_total)
    near, far = both_cores(*parts)
    query_total = Task(plan.reduce_all(near, far, small=True)).go(1)
    pack_total.go(1)
    last_idx = after(idx, far)
    terms = totals[0]
    stacked = ((nd * take, 2 * KW + 128), BF16)
    grad_tokens, *parts = call(
        functools.partial(last_kernel, nd, len(terms)),
        "last",
        [((model, count), BF16), stacked, stacked],
        [last_idx, x, gains, cos, sin, normed, gq, w_full, grad_mid] + terms,
        smem=1,
        scratch=[pltpu.VMEM((width + 64, count), BF16), pltpu.VMEM((model, 128), BF16)],
        limit=28,
        us=6,
    )
    plan.gates = (parts[0],)
    out_got = plan.swap(sums[1])
    output = (mid + (sums[0].astype(F32) + out_got.astype(F32))).astype(BF16)
    kv_total = Task(plan.reduce_all(*both_cores(*parts), small=True))
    packs = list(pack_total.finish())
    gate, up, down = call(
        functools.partial(unpack_kernel, nd),
        "unpack",
        [(w.shape, F32) for w in (w_gate, w_up, w_down.T)],
        packs,
        limit=24,
        us=6,
    )
    kv_total.go(plan.kd + plan.kz)
    query_total.go(plan.kd - 1 + plan.kz)
    plan.gates = (up,)
    kv_halves = kv_total.finish()
    query_halves = query_total.finish()

    qkv_whole, out_whole, mlp_gain, attn_gain = call(
        final_kernel,
        "final",
        [
            ((shard, width), F32),
            ((shard, model), F32),
            ((1, shard), F32),
            ((1, shard), F32),
        ],
        list(query_halves) + list(kv_halves),
        limit=12,
        us=2,
    )
    return (
        output.T[None],
        grad_tokens.T[None],
        qkv_whole,
        out_whole,
        gate,
        up,
        down.T,
        attn_gain[0],
        mlp_gain[0],
    )


def solution(mesh):
    rows = P("dp", None)
    stored = P("dp", "ctx", None)
    vector = P("dp")
    return jax.shard_map(
        functools.partial(local, mesh.shape["dp"], mesh.shape["ctx"]),
        mesh=mesh,
        in_specs=(stored, P("dp", "ctx"), rows, rows, rows, rows, rows, vector, vector, stored),
        out_specs=(stored, stored, rows, rows, rows, rows, rows, vector, vector),
        check_vma=False,
    )
```
